32 devices in a mesh: seq: 8 (over y, x, core), tp: 4 (over z).
Axes of the slice: x: 2, y: 2, z: 4, core: 2. Of those that a mesh axis runs over, the one named last changes fastest.
Arguments:
- tokens: bfloat16 [1024, 4096], P('seq', 'tp'), may hold values from -6 to 6
- in_weight: bfloat16 [4096, 8192], P(None, 'tp'), may hold values from -0.09375 to 0.09375
- conv_weight: float32 [4, 8192], P(None, 'tp'), may hold values from -3 to 3
- conv_bias: float32 [8192], P('tp'), may hold values from -0.5 to 0.5
- proj_weight: bfloat16 [8192, 288], P('tp'), may hold values from -0.0625 to 0.0625
- dt_weight: bfloat16 [256, 8192], P(None, 'tp'), may hold values from -0.375 to 0.375
- dt_bias: float32 [8192], P('tp'), may hold values from -7 to -2
- a_log: float32 [16, 8192], P(None, 'tp'), may hold values from -3 to 1.5
- skip_gain: float32 [8192], P('tp'), may hold values from 0.5 to 1.5
- threshold: float32 [8192], P('tp'), may hold values from -0.5 to 0.5
Outputs:
- gated: bfloat16 [1024, 8192], P('seq', 'tp')
The draws below stay inside these ranges and needn't reach their ends.
All inputs are finite; a program needn't handle non-finite values.
Results may differ from the reference program's by a relative error of at most 0.0085.
Values may be sent and summed in bfloat16 or wider, within the bound.
A program may use at most 64 MiB of HBM per device.

```python
import jax
import jax.numpy as jnp
from jax import lax

D = 4096
DI = 8192
N = 16
R = 256
CONV = 4
TOKENS = 1024


def shard_levels(stream_key, shape, shards, smallest, high):
    def one(axis_at, shards_of):
        draws = jax.random.uniform(jax.random.fold_in(jax.random.fold_in(stream_key, 6), axis_at), (shards_of,), jnp.float32, smallest / len(shards), high / len(shards))
        return jnp.repeat(jnp.exp(draws), shape[axis_at] // shards_of).reshape((-1,) + (1,) * (len(shape) - axis_at - 1))

    loudness = one(*shards[0])
    for cut in shards[1:]:
        loudness = loudness * one(*cut)
    return loudness


def normal_values(key, shape, deviation, limit, split=(), dtype=jnp.bfloat16):
    drawn = deviation * jax.random.normal(key, shape, jnp.float32)
    if split:
        drawn = drawn * shard_levels(key, shape, split, -0.22, 0.18)
    return jnp.clip(drawn, -limit, limit).astype(dtype)


def setup_inputs(seed: int = 0) -> dict:
    splits = jax.random.split(jax.random.key(seed), 11)
    tokens = normal_values(splits[0], (TOKENS, D), 1.0, 6.0, ((0, 8), (1, 4)))
    in_weight = normal_values(splits[1], (D, DI), D ** -0.5, 0.09375, ((1, 4),))
    conv_weight = normal_values(splits[2], (CONV, DI), CONV ** -0.5, 3.0, ((1, 4),), jnp.float32)
    conv_bias = jnp.clip(jax.random.uniform(splits[3], (DI,), jnp.float32, -0.5, 0.5) * shard_levels(splits[3], (DI,), ((0, 4),), -0.4, 0.0), -0.5, 0.5)
    proj_weight = normal_values(splits[4], (DI, R + 2 * N), DI ** -0.5, 0.0625, ((0, 4),))
    dt_weight = normal_values(splits[5], (R, DI), R ** -0.5, 0.375, ((1, 4),))
    dt_bias = jnp.clip(-7.0 + 5.0 * jax.random.uniform(splits[6], (DI,), jnp.float32) ** shard_levels(splits[6], (DI,), ((0, 4),), -0.2, 0.2), -7.0, -2.0)
    a_log = jnp.clip(-3.0 + 4.5 * jax.random.uniform(splits[7], (N, DI), jnp.float32) ** shard_levels(splits[7], (N, DI), ((1, 4),), -0.2, 0.2), -3.0, 1.5)
    skip_gain = jnp.clip(0.5 + 1.0 * jax.random.uniform(splits[8], (DI,), jnp.float32) ** shard_levels(splits[8], (DI,), ((0, 4),), -0.2, 0.2), 0.5, 1.5)
    threshold = jnp.clip(jax.random.uniform(splits[9], (DI,), jnp.float32, -0.5, 0.5) * shard_levels(splits[9], (DI,), ((0, 4),), -0.4, 0.0), -0.5, 0.5)
    return {"tokens": tokens, "in_weight": in_weight, "conv_weight": conv_weight, "conv_bias": conv_bias, "proj_weight": proj_weight, "dt_weight": dt_weight, "dt_bias": dt_bias, "a_log": a_log, "skip_gain": skip_gain, "threshold": threshold}


def reference(tokens, in_weight, conv_weight, conv_bias, proj_weight, dt_weight, dt_bias, a_log, skip_gain, threshold):
    inner = jnp.dot(tokens, in_weight, preferred_element_type=jnp.float32).astype(jnp.bfloat16)
    padded = jnp.concatenate([jnp.zeros((CONV - 1, DI), jnp.bfloat16), inner], axis=0)
    pre = conv_bias[None, :] + jnp.zeros((TOKENS, DI), jnp.float32)
    for k in range(CONV):
        pre = pre + conv_weight[k][None, :] * padded[k:k + TOKENS].astype(jnp.float32)
    u = jax.nn.silu(pre).astype(jnp.bfloat16)
    total = jnp.dot(u, proj_weight, preferred_element_type=jnp.float32)
    dt_low = total[:, :R].astype(jnp.bfloat16)
    b_coef = total[:, R:R + N]
    c_coef = total[:, R + N:]
    dt = jax.nn.softplus(jnp.dot(dt_low, dt_weight, preferred_element_type=jnp.float32) + dt_bias[None, :])
    rate = -jnp.exp(a_log)
    u_float = u.astype(jnp.float32)

    def advance(state, items):
        dt_row, u_row, b_row, c_row = items
        state = jnp.exp(dt_row[None, :] * rate) * state + (dt_row * u_row)[None, :] * b_row[:, None]
        return state, jnp.sum(c_row[:, None] * state, axis=0)

    start = jnp.zeros((N, DI), jnp.float32)
    _, scanned = lax.scan(advance, start, (dt, u_float, b_coef, c_coef))
    y_full = scanned + skip_gain[None, :] * u_float
    return (y_full * jax.nn.sigmoid(4.0 * (y_full - threshold[None, :]))).astype(jnp.bfloat16)
```

```python
import functools

import jax
import jax.numpy as jnp
from jax import lax
from jax.experimental import pallas as pl
from jax.experimental.pallas import tpu as pltpu
from jax.sharding import PartitionSpec as P

MESH = pl.DeviceIdType.MESH
LOG2E = 1.4426950408889634
LANES = 128
HALVES = 2


def kernel(
    ns,
    ntp,
    tok_ref,
    w_hbm,
    cw_ref,
    cb_ref,
    proj_ref,
    dtw_ref,
    dtb_ref,
    alog_ref,
    skip_ref,
    thr_ref,
    out_ref,
    w_ref,
    tok_all,
    acc,
    pad,
    halo_out,
    halo_in,
    u_ref,
    part,
    ps,
    rs,
    ag,
    tot,
    bs,
    dt3,
    du3,
    y3,
    r3,
    sx,
    sr,
    entry,
    w_sem,
    tok_recv,
    tok_right,
    tok_left,
    halo_sem,
    rs_send,
    rs_recv,
    ag_send,
    ag_recv,
    st_send,
    st_recv,
):
    q = lax.axis_index("seq")
    z = lax.axis_index("tp")
    rows, depth = tok_ref.shape
    width = w_ref.shape[1]
    taps = cw_ref.shape[0]
    rank = dtw_ref.shape[0]
    n_state = alog_ref.shape[0]
    cols = proj_ref.shape[1]
    tiles = width // LANES
    stride = r3.shape[0] // n_state
    groups = stride // 8
    piece = rows // HALVES
    per = rows // ntp
    f32, bf16 = jnp.float32, jnp.bfloat16

    def w_copy(k):
        part_k = pl.ds(pl.multiple_of(k * depth, depth), depth)
        return pltpu.make_async_copy(w_hbm.at[part_k], w_ref.at[part_k], w_sem.at[k])

    for i in range(ntp):
        w_copy(lax.rem(z + i, ntp)).start()

    barrier = pltpu.get_barrier_semaphore()
    for d in range(1, ntp):
        pl.semaphore_signal(
            barrier, inc=1, device_id={"tp": lax.rem(z + d, ntp)}, device_id_type=MESH
        )
    for d in range(1, ns):
        pl.semaphore_signal(
            barrier, inc=1, device_id={"seq": lax.rem(q + d, ns)}, device_id_type=MESH
        )
    pl.semaphore_wait(barrier, ns + ntp - 2)

    def tok_copy(k, h, by, sems, own):
        at = pl.ds(h * piece, piece)
        return pltpu.make_async_remote_copy(
            src_ref=tok_ref.at[at] if own else tok_all.at[k, at],
            dst_ref=tok_all.at[k, at],
            send_sem=sems.at[k, h],
            recv_sem=tok_recv.at[k, h],
            device_id={"tp": z + by},
            device_id_type=MESH,
        )

    for h in range(HALVES):

        @pl.when(z + 1 < ntp)
        def _():
            tok_copy(z, h, 1, tok_right, True).start()

        @pl.when(z > 0)
        def _():
            tok_copy(z, h, -1, tok_left, True).start()

    tn = min(512, width)

    def multiply(block, k, first):
        w_copy(k).wait()
        part_k = pl.ds(pl.multiple_of(k * depth, depth), depth)

        @pl.loop(0, width // tn)
        def _(i):
            at = pl.ds(pl.multiple_of(i * tn, tn), tn)
            got = jnp.dot(block[...], w_ref[part_k, at], preferred_element_type=f32)
            acc[:, at] = got if first else acc[:, at] + got

    for j in range(tiles):
        at = slice(j * LANES, (j + 1) * LANES)
        r3[pl.ds(j, n_state, stride=stride), :] = -LOG2E * jnp.exp(alog_ref[:, at])
    multiply(tok_ref, z, True)

    for d in range(1, ntp):
        for h in range(HALVES):

            @pl.when(z - d >= 0)
            def _():
                tok_copy(z - d, h, 1, tok_right, False).wait_recv()

                @pl.when(z + 1 < ntp)
                def _():
                    tok_copy(z - d, h, 1, tok_right, False).start()

            @pl.when(z + d < ntp)
            def _():
                tok_copy(z + d, h, -1, tok_left, False).wait_recv()

                @pl.when(z > 0)
                def _():
                    tok_copy(z + d, h, -1, tok_left, False).start()

        @pl.when(z - d >= 0)
        def _():
            multiply(tok_all.at[z - d], z - d, False)

        @pl.when(z + d < ntp)
        def _():
            multiply(tok_all.at[z + d], z + d, False)

    halo_out[...] = acc[rows - 16 :, :].astype(bf16)
    halo = pltpu.make_async_remote_copy(
        src_ref=halo_out,
        dst_ref=halo_in,
        send_sem=halo_sem.at[0],
        recv_sem=halo_sem.at[1],
        device_id={"seq": q + 1},
        device_id_type=MESH,
    )

    @pl.when(q + 1 < ns)
    def _():
        halo.start()

    pad[pl.ds(8, rows), :] = acc[...].astype(bf16).astype(f32)

    @pl.when(q > 0)
    def _():
        halo.wait_recv()
        pad[pl.ds(0, 8), :] = halo_in[...].astype(f32)[8:]

    @pl.when(q == 0)
    def _():
        pad[pl.ds(0, 8), :] = jnp.zeros((8, width), f32)

    for j in range(tiles):
        at = slice(j * LANES, (j + 1) * LANES)
        pre = cb_ref[:, at] + cw_ref[0:1, at] * pad[pl.ds(9 - taps, rows), at]
        for k in range(1, taps):
            pre = pre + cw_ref[k : k + 1, at] * pad[pl.ds(9 - taps + k, rows), at]
        u_ref[:, at] = (pre / (1.0 + jnp.exp(-pre))).astype(bf16)

    part[:, :cols] = jnp.dot(u_ref[...], proj_ref[...], preferred_element_type=f32)
    part[:, cols:] = jnp.zeros((rows, part.shape[1] - cols), f32)
    for k in range(ntp):
        ps[k] = part[k * per : (k + 1) * per, :].astype(bf16)

    def rs_copy(d):
        to = lax.rem(z + d, ntp)
        return pltpu.make_async_remote_copy(
            src_ref=ps.at[to],
            dst_ref=rs.at[d - 1],
            send_sem=rs_send.at[d - 1],
            recv_sem=rs_recv.at[d - 1],
            device_id={"tp": to},
            device_id_type=MESH,
        )

    def ag_copy(d):
        to = lax.rem(z + d, ntp)
        return pltpu.make_async_remote_copy(
            src_ref=ag.at[z],
            dst_ref=ag.at[z],
            send_sem=ag_send.at[d - 1],
            recv_sem=ag_recv.at[d - 1],
            device_id={"tp": to},
            device_id_type=MESH,
        )

    for d in range(1, ntp):
        rs_copy(d).start()
    red = part[pl.ds(pl.multiple_of(z * per, per), per), :]
    for d in range(1, ntp):
        rs_copy(d).wait_recv()
        red = red + rs[d - 1].astype(f32)
    ag[z] = red.astype(bf16)
    for d in range(1, ntp):
        ag_copy(d).start()
    for d in range(1, ntp):
        ag_copy(d).wait_recv()
    for k in range(ntp):
        tot[pl.ds(k * per, per), :] = ag[k].astype(f32)

    dt_low = tot[:, :rank].astype(bf16)
    for j0 in range(0, width, tn):
        at = slice(j0, j0 + tn)
        v = jnp.dot(dt_low, dtw_ref[:, at], preferred_element_type=f32) + dtb_ref[:, at]
        v = jnp.maximum(v, 0.0) + jnp.log1p(jnp.exp(-jnp.abs(v)))
        flow = v * u_ref[:, at].astype(f32)
        for i in range(tn // LANES):
            cut = slice(i * LANES, (i + 1) * LANES)
            to = pl.ds(j0 // LANES + i, rows, stride=stride)
            dt3[to, :] = v[:, cut]
            du3[to, :] = flow[:, cut]
    two = 2 * n_state
    for n in range(two):
        bs[pl.ds(n, rows, stride=two), :] = jnp.broadcast_to(
            tot[:, rank + n : rank + n + 1], (rows, LANES)
        )

    def rates(g):
        return [r3[pl.ds(n * stride + g * 8, 8), :] for n in range(n_state)]

    def splat(t, n):
        return jnp.broadcast_to(bs[pl.ds(t * two + n, 1), :], (8, LANES))

    def st_copy(g, d):
        return pltpu.make_async_remote_copy(
            src_ref=sx.at[g],
            dst_ref=sr.at[g, d - 1],
            send_sem=st_send.at[g, d - 1],
            recv_sem=st_recv.at[g, d - 1],
            device_id={"seq": q + d},
            device_id_type=MESH,
        )

    def first_pass(g):
        rate = rates(g)

        def step(t, carry):
            states, total = carry
            at = pl.ds(pl.multiple_of(t * stride + g * 8, 8), 8)
            dt, du = dt3[at, :], du3[at, :]
            states = [
                jnp.exp2(dt * rate[n]) * states[n] + du * splat(t, n) for n in range(n_state)
            ]
            return states, total + dt

        zero = jnp.zeros((8, LANES), f32)
        states, total = lax.fori_loop(0, rows, step, ([zero] * n_state, zero), unroll=4)
        high = total.astype(bf16).astype(f32)
        items = states + [high, total - high]
        for n in range(0, len(items), 2):
            sx[g, pl.ds(n * 8, 16), :] = jnp.concatenate(items[n : n + 2], axis=0).astype(bf16)
        for d in range(1, ns):

            @pl.when(q + d < ns)
            def _():
                st_copy(g, d).start()

    def second_pass(g):
        rate = rates(g)
        zero = jnp.zeros((8, LANES), f32)
        for n in range(n_state):
            entry[pl.ds(n * 8, 8), :] = zero
        for d in range(ns - 1, 0, -1):

            @pl.when(q - d >= 0)
            def _():
                st_copy(g, d).wait_recv()
                sums = sr[g, d - 1, pl.ds(n_state * 8, 16), :].astype(f32)
                sums = sums[:8] + sums[8:]
                for n in range(0, n_state, 2):
                    ends = sr[g, d - 1, pl.ds(n * 8, 16), :].astype(f32)
                    for i in range(2):
                        at = pl.ds((n + i) * 8, 8)
                        entry[at, :] = (
                            jnp.exp2(sums * rate[n + i]) * entry[at, :] + ends[i * 8 : i * 8 + 8]
                        )

        def step(t, states):
            at = pl.ds(pl.multiple_of(t * stride + g * 8, 8), 8)
            dt, du = dt3[at, :], du3[at, :]
            states = [
                jnp.exp2(dt * rate[n]) * states[n] + du * splat(t, n) for n in range(n_state)
            ]
            terms = [splat(t, n_state + n) * states[n] for n in range(n_state)]
            while len(terms) > 1:
                terms = [a + b for a, b in zip(terms[::2], terms[1::2])]
            y3[at, :] = terms[0]
            return states

        lax.fori_loop(0, rows, step, [entry[pl.ds(n * 8, 8), :] for n in range(n_state)], unroll=4)

    for g in range(groups):
        first_pass(g)
    for g in range(groups):
        second_pass(g)
        for j in range(g * 8, min(g * 8 + 8, tiles)):
            at = slice(j * LANES, (j + 1) * LANES)
            y = y3[pl.ds(j, rows, stride=stride), :] + skip_ref[:, at] * u_ref[:, at].astype(f32)
            out_ref[:, at] = (y / (1.0 + jnp.exp(-4.0 * (y - thr_ref[:, at])))).astype(bf16)

    for k in range(ntp):
        for h in range(HALVES):

            @pl.when((z + 1 < ntp) & (k <= z))
            def _():
                tok_copy(k, h, 1, tok_right, False).wait_send()

            @pl.when((z > 0) & (k >= z))
            def _():
                tok_copy(k, h, -1, tok_left, False).wait_send()

    @pl.when(q + 1 < ns)
    def _():
        halo.wait_send()

    for d in range(1, ntp):
        rs_copy(d).wait_send()
        ag_copy(d).wait_send()
    for g in range(groups):
        for d in range(1, ns):

            @pl.when(q + d < ns)
            def _():
                st_copy(g, d).wait_send()


def per_device(
    ns,
    ntp,
    tokens,
    in_weight,
    conv_weight,
    conv_bias,
    proj_weight,
    dt_weight,
    dt_bias,
    a_log,
    skip_gain,
    threshold,
):
    rows, depth = tokens.shape
    width = in_weight.shape[1]
    n_state = a_log.shape[0]
    stride = -(-width // (8 * LANES)) * 8
    groups = stride // 8
    padded = -(-proj_weight.shape[1] // LANES) * LANES
    per = rows // ntp
    f32, bf16 = jnp.float32, jnp.bfloat16
    dma = pltpu.SemaphoreType.DMA
    vmem = pl.BlockSpec(memory_space=pltpu.VMEM)
    return pl.pallas_call(
        functools.partial(kernel, ns, ntp),
        out_shape=jax.ShapeDtypeStruct((rows, width), bf16),
        in_specs=[vmem, pl.BlockSpec(memory_space=pl.ANY)] + [vmem] * 8,
        out_specs=vmem,
        scratch_shapes=[
            pltpu.VMEM(in_weight.shape, bf16),
            pltpu.VMEM((ntp, rows, depth), bf16),
            pltpu.VMEM((rows, width), f32),
            pltpu.VMEM((rows + 8, width), f32),
            pltpu.VMEM((16, width), bf16),
            pltpu.VMEM((16, width), bf16),
            pltpu.VMEM((rows, width), bf16),
            pltpu.VMEM((rows, padded), f32),
            pltpu.VMEM((ntp, per, padded), bf16),
            pltpu.VMEM((ntp - 1, per, padded), bf16),
            pltpu.VMEM((ntp, per, padded), bf16),
            pltpu.VMEM((rows, padded), f32),
            pltpu.VMEM((rows * 2 * n_state, LANES), f32),
            pltpu.VMEM((rows * stride, LANES), f32),
            pltpu.VMEM((rows * stride, LANES), f32),
            pltpu.VMEM((rows * stride, LANES), f32),
            pltpu.VMEM((n_state * stride, LANES), f32),
            pltpu.VMEM((groups, n_state * 8 + 16, LANES), bf16),
            pltpu.VMEM((groups, ns - 1, n_state * 8 + 16, LANES), bf16),
            pltpu.VMEM((n_state * 8, LANES), f32),
            dma((ntp,)),
            dma((ntp, HALVES)),
            dma((ntp, HALVES)),
            dma((ntp, HALVES)),
            dma((2,)),
            dma((ntp - 1,)),
            dma((ntp - 1,)),
            dma((ntp - 1,)),
            dma((ntp - 1,)),
            dma((groups, ns - 1)),
            dma((groups, ns - 1)),
        ],
        compiler_params=pltpu.CompilerParams(
            collective_id=0, has_side_effects=True, vmem_limit_bytes=48 * 1024 * 1024
        ),
    )(
        tokens,
        in_weight,
        conv_weight,
        conv_bias.reshape(1, -1),
        proj_weight,
        dt_weight,
        dt_bias.reshape(1, -1),
        a_log,
        skip_gain.reshape(1, -1),
        threshold.reshape(1, -1),
    )


def solution(mesh):
    return jax.shard_map(
        functools.partial(per_device, mesh.shape["seq"], mesh.shape["tp"]),
        mesh=mesh,
        in_specs=(
            P("seq", "tp"),
            P(None, "tp"),
            P(None, "tp"),
            P("tp"),
            P("tp", None),
            P(None, "tp"),
            P("tp"),
            P(None, "tp"),
            P("tp"),
            P("tp"),
        ),
        out_specs=P("seq", "tp"),
        check_vma=False,
    )
```

```python
import functools

import jax
import jax.numpy as jnp
from jax import lax
from jax.experimental import pallas as pl
from jax.experimental.pallas import tpu as pltpu
from jax.sharding import PartitionSpec as P

MESH = pl.DeviceIdType.MESH
LOG2E = 1.4426950408889634
LANES = 128


def kernel(
    ns,
    ntp,
    tok_hbm,
    w_hbm,
    cw_hbm,
    cb_hbm,
    proj_hbm,
    dtw_hbm,
    dtb_hbm,
    alog_hbm,
    skip_hbm,
    thr_hbm,
    out_ref,
    w_ref,
    cw_ref,
    cb_ref,
    proj_ref,
    dtw_ref,
    dtb_ref,
    alog_ref,
    skip_ref,
    thr_ref,
    tok_all,
    acc,
    pad,
    halo_out,
    halo_in,
    u_ref,
    part,
    ps,
    rs,
    ag,
    tot,
    bs,
    dt3,
    du3,
    y3,
    r3,
    later,
    sx,
    sr,
    entry,
    w_sem,
    in_sem,
    tok_recv,
    tok_right,
    tok_left,
    halo_sem,
    rs_send,
    rs_recv,
    ag_send,
    ag_recv,
    st_send,
    st_recv,
):
    q = lax.axis_index("seq")
    z = lax.axis_index("tp")
    rows, depth = tok_hbm.shape
    width = w_ref.shape[1]
    taps = cw_ref.shape[0]
    rank = dtw_ref.shape[0]
    n_state = alog_ref.shape[0]
    cols = proj_ref.shape[0]
    tiles = width // LANES
    stride = r3.shape[0] // n_state
    groups = stride // 8
    per = ag.shape[2]
    f32, bf16 = jnp.float32, jnp.bfloat16
    half = rows // 2
    split = half - 16
    token_rows = ((split, rows - split), (0, split))
    phase_rows = (half, 0)

    small = [
        (cw_hbm, cw_ref),
        (cb_hbm, cb_ref),
        (proj_hbm, proj_ref),
        (dtw_hbm, dtw_ref),
        (dtb_hbm, dtb_ref),
        (alog_hbm, alog_ref),
        (skip_hbm, skip_ref),
        (thr_hbm, thr_ref),
        (tok_hbm, tok_all.at[z]),
    ]

    def in_copy(i):
        return pltpu.make_async_copy(small[i][0], small[i][1], in_sem.at[i])

    def w_copy(k):
        part_k = pl.ds(pl.multiple_of(k * depth, depth), depth)
        return pltpu.make_async_copy(w_hbm.at[part_k], w_ref.at[part_k], w_sem.at[k])

    in_copy(8).start()
    w_copy(z).start()

    barrier = pltpu.get_barrier_semaphore()
    for d in range(1, ntp):
        pl.semaphore_signal(
            barrier, inc=1, device_id={"tp": lax.rem(z + d, ntp)}, device_id_type=MESH
        )
    for d in range(1, ns):
        pl.semaphore_signal(
            barrier, inc=1, device_id={"seq": lax.rem(q + d, ns)}, device_id_type=MESH
        )
    for i in (5, 0, 1, 2, 3, 4, 6, 7):
        in_copy(i).start()
    for i in range(1, ntp):
        w_copy(lax.rem(z + i, ntp)).start()
    pl.semaphore_wait(barrier, ns + ntp - 2)

    def tok_copy(k, h, by, sems, own):
        at = pl.ds(*token_rows[h])
        return pltpu.make_async_remote_copy(
            src_ref=tok_hbm.at[at] if own else tok_all.at[k, at],
            dst_ref=tok_all.at[k, at],
            send_sem=sems.at[k, h],
            recv_sem=tok_recv.at[k, h],
            device_id={"tp": z + by},
            device_id_type=MESH,
        )

    def send_own(h):
        @pl.when(z + 1 < ntp)
        def _():
            tok_copy(z, h, 1, tok_right, True).start()

        @pl.when(z > 0)
        def _():
            tok_copy(z, h, -1, tok_left, True).start()

    def take(d, h):
        @pl.when(z - d >= 0)
        def _():
            tok_copy(z - d, h, 1, tok_right, False).wait_recv()

            @pl.when(z + 1 < ntp)
            def _():
                tok_copy(z - d, h, 1, tok_right, False).start()

        @pl.when(z + d < ntp)
        def _():
            tok_copy(z + d, h, -1, tok_left, False).wait_recv()

            @pl.when(z > 0)
            def _():
                tok_copy(z + d, h, -1, tok_left, False).start()

    tn = min(512, width)

    def multiply(k, h, first):
        if h == 0:
            w_copy(k).wait()
        part_k = pl.ds(pl.multiple_of(k * depth, depth), depth)
        mine = pl.ds(*token_rows[h])

        @pl.loop(0, width // tn)
        def _(i):
            at = pl.ds(pl.multiple_of(i * tn, tn), tn)
            got = jnp.dot(tok_all[k, mine, :], w_ref[part_k, at], preferred_element_type=f32)
            acc[mine, at] = got if first else acc[mine, at] + got

    def multiply_pair(d, h):
        @pl.when(z - d >= 0)
        def _():
            multiply(z - d, h, False)

        @pl.when(z + d < ntp)
        def _():
            multiply(z + d, h, False)

    halo = pltpu.make_async_remote_copy(
        src_ref=halo_out,
        dst_ref=halo_in,
        send_sem=halo_sem.at[0],
        recv_sem=halo_sem.at[1],
        device_id={"seq": q + 1},
        device_id_type=MESH,
    )

    def rs_copy(p, d):
        to = lax.rem(z + d, ntp)
        return pltpu.make_async_remote_copy(
            src_ref=ps.at[p, to],
            dst_ref=rs.at[p, d - 1],
            send_sem=rs_send.at[p, d - 1],
            recv_sem=rs_recv.at[p, d - 1],
            device_id={"tp": to},
            device_id_type=MESH,
        )

    def ag_copy(p, d):
        to = lax.rem(z + d, ntp)
        return pltpu.make_async_remote_copy(
            src_ref=ag.at[p, z],
            dst_ref=ag.at[p, z],
            send_sem=ag_send.at[p, d - 1],
            recv_sem=ag_recv.at[p, d - 1],
            device_id={"tp": to},
            device_id_type=MESH,
        )

    def project(p):
        r0 = phase_rows[p]
        for j in range(tiles):
            at = slice(j * LANES, (j + 1) * LANES)
            pre = cb_ref[:, at] + cw_ref[0:1, at] * pad[pl.ds(r0 + 9 - taps, half), at]
            for k in range(1, taps):
                pre = pre + cw_ref[k : k + 1, at] * pad[pl.ds(r0 + 9 - taps + k, half), at]
            u_ref[pl.ds(r0, half), at] = (pre / (1.0 + jnp.exp(-pre))).astype(bf16)
        sums = lax.dot_general(
            u_ref[pl.ds(r0, half), :],
            proj_ref[...],
            (((1,), (1,)), ((), ())),
            preferred_element_type=f32,
        )
        for k in range(ntp):
            mine = sums[k * per : (k + 1) * per]
            part[p, k, :, :cols] = mine
            ps[p, k, :, :cols] = mine.astype(ps.dtype)
        for d in range(1, ntp):
            rs_copy(p, d).start()

    def reduce(p):
        red = part[p, z]
        for d in range(1, ntp):
            rs_copy(p, d).wait_recv()
            red = red + rs[p, d - 1].astype(f32)
        ag[p, z] = red.astype(ag.dtype)
        for d in range(1, ntp):
            ag_copy(p, d).start()

    two = 2 * n_state

    def prepare(p):
        r0 = phase_rows[p]
        mine = pl.ds(r0, half)
        for d in range(1, ntp):
            ag_copy(p, d).wait_recv()
        for k in range(ntp):
            tot[pl.ds(r0 + k * per, per), :] = ag[p, k].astype(f32)
        dt_low = tot[mine, :rank].astype(bf16)
        for j0 in range(0, width, tn):
            at = slice(j0, j0 + tn)
            v = jnp.dot(dt_low, dtw_ref[:, at], preferred_element_type=f32) + dtb_ref[:, at]
            v = jnp.maximum(v, 0.0) + jnp.log1p(jnp.exp(-jnp.abs(v)))
            flow = v * u_ref[mine, at].astype(f32)
            for i in range(tn // LANES):
                cut = slice(i * LANES, (i + 1) * LANES)
                to = pl.ds(r0 * stride + j0 // LANES + i, half, stride=stride)
                dt3[to, :] = v[:, cut]
                du3[to, :] = flow[:, cut]
        for n in range(two):
            bs[pl.ds(r0 * two + n, half, stride=two), :] = jnp.broadcast_to(
                tot[mine, rank + n : rank + n + 1], (half, LANES)
            )

    def rates(g):
        return [r3[pl.ds(n * stride + g * 8, 8), :] for n in range(n_state)]

    def splat(t, n):
        return jnp.broadcast_to(bs[pl.ds(t * two + n, 1), :], (8, LANES))

    def st_copy(g, d):
        return pltpu.make_async_remote_copy(
            src_ref=sx.at[g],
            dst_ref=sr.at[g, d - 1],
            send_sem=st_send.at[g, d - 1],
            recv_sem=st_recv.at[g, d - 1],
            device_id={"seq": q + d},
            device_id_type=MESH,
        )

    def first_pass(p, g):
        rate = rates(g)
        r0 = phase_rows[p]

        def step(t, carry):
            states, total = carry
            at = pl.ds(pl.multiple_of(t * stride + g * 8, 8), 8)
            dt, du = dt3[at, :], du3[at, :]
            states = [
                jnp.exp2(dt * rate[n]) * states[n] + du * splat(t, n) for n in range(n_state)
            ]
            return states, total + dt

        zero = jnp.zeros((8, LANES), f32)
        states, total = lax.fori_loop(
            r0, r0 + half, step, ([zero] * n_state, zero), unroll=4
        )
        if p == 0:
            for n in range(n_state):
                later[g, pl.ds(n * 8, 8), :] = states[n]
            later[g, pl.ds(n_state * 8, 8), :] = total
            return
        more = later[g, pl.ds(n_state * 8, 8), :]
        states = [
            jnp.exp2(more * rate[n]) * states[n] + later[g, pl.ds(n * 8, 8), :]
            for n in range(n_state)
        ]
        total = total + more
        high = total.astype(bf16).astype(f32)
        items = states + [high, total - high]
        for n in range(0, len(items), 2):
            sx[g, pl.ds(n * 8, 16), :] = jnp.concatenate(items[n : n + 2], axis=0).astype(bf16)
        for d in range(1, ns):

            @pl.when(q + d < ns)
            def _():
                st_copy(g, d).start()

    def second_pass(g):
        rate = rates(g)
        zero = jnp.zeros((8, LANES), f32)
        for n in range(n_state):
            entry[pl.ds(n * 8, 8), :] = zero
        for d in range(ns - 1, 0, -1):

            @pl.when(q - d >= 0)
            def _():
                st_copy(g, d).wait_recv()
                sums = sr[g, d - 1, pl.ds(n_state * 8, 16), :].astype(f32)
                sums = sums[:8] + sums[8:]
                for n in range(0, n_state, 2):
                    ends = sr[g, d - 1, pl.ds(n * 8, 16), :].astype(f32)
                    for i in range(2):
                        at = pl.ds((n + i) * 8, 8)
                        entry[at, :] = (
                            jnp.exp2(sums * rate[n + i]) * entry[at, :] + ends[i * 8 : i * 8 + 8]
                        )

        def step(t, states):
            at = pl.ds(pl.multiple_of(t * stride + g * 8, 8), 8)
            dt, du = dt3[at, :], du3[at, :]
            states = [
                jnp.exp2(dt * rate[n]) * states[n] + du * splat(t, n) for n in range(n_state)
            ]
            terms = [splat(t, n_state + n) * states[n] for n in range(n_state)]
            while len(terms) > 1:
                terms = [a + b for a, b in zip(terms[::2], terms[1::2])]
            y3[at, :] = terms[0]
            return states

        lax.fori_loop(0, rows, step, [entry[pl.ds(n * 8, 8), :] for n in range(n_state)], unroll=4)
        for j in range(g * 8, min(g * 8 + 8, tiles)):
            at = slice(j * LANES, (j + 1) * LANES)
            y = y3[pl.ds(j, rows, stride=stride), :] + skip_ref[:, at] * u_ref[:, at].astype(f32)
            out_ref[:, at] = (y / (1.0 + jnp.exp(-4.0 * (y - thr_ref[:, at])))).astype(bf16)

    send_own(0)
    in_copy(8).wait()
    in_copy(5).wait()
    for j in range(tiles):
        at = slice(j * LANES, (j + 1) * LANES)
        r3[pl.ds(j, n_state, stride=stride), :] = -LOG2E * jnp.exp(alog_ref[:, at])
    part[:, :, :, cols:] = jnp.zeros(part.shape[:3] + (part.shape[3] - cols,), f32)
    ps[:, :, :, cols:] = jnp.zeros(ps.shape[:3] + (ps.shape[3] - cols,), ps.dtype)
    send_own(1)
    multiply(z, 0, True)
    for d in range(1, ntp):
        take(d, 0)
        multiply_pair(d, 0)
        if d < ntp - 1:
            take(d, 1)
    halo_out[...] = acc[rows - 16 :, :].astype(bf16)

    @pl.when(q + 1 < ns)
    def _():
        halo.start()

    pad[pl.ds(8 + split, rows - split), :] = acc[split:, :].astype(bf16).astype(f32)
    for i in (0, 1, 2):
        in_copy(i).wait()
    project(0)

    multiply(z, 1, True)
    for d in range(1, ntp - 1):
        multiply_pair(d, 1)
    reduce(0)
    if ntp > 1:
        take(ntp - 1, 1)
        multiply_pair(ntp - 1, 1)
    pad[pl.ds(8, split), :] = acc[:split, :].astype(bf16).astype(f32)

    @pl.when(q > 0)
    def _():
        halo.wait_recv()
        pad[pl.ds(0, 8), :] = halo_in[...].astype(f32)[8:]

    @pl.when(q == 0)
    def _():
        pad[pl.ds(0, 8), :] = jnp.zeros((8, width), f32)

    project(1)

    in_copy(3).wait()
    in_copy(4).wait()
    prepare(0)
    reduce(1)
    for g in range(groups):
        first_pass(0, g)
    prepare(1)
    for g in range(groups):
        first_pass(1, g)
    in_copy(6).wait()
    in_copy(7).wait()
    for g in range(groups):
        second_pass(g)

    for k in range(ntp):
        for h in range(2):

            @pl.when((z + 1 < ntp) & (k <= z))
            def _():
                tok_copy(k, h, 1, tok_right, False).wait_send()

            @pl.when((z > 0) & (k >= z))
            def _():
                tok_copy(k, h, -1, tok_left, False).wait_send()

    @pl.when(q + 1 < ns)
    def _():
        halo.wait_send()

    for p in range(2):
        for d in range(1, ntp):
            rs_copy(p, d).wait_send()
            ag_copy(p, d).wait_send()
    for g in range(groups):
        for d in range(1, ns):

            @pl.when(q + d < ns)
            def _():
                st_copy(g, d).wait_send()


def per_device(
    ns,
    ntp,
    tokens,
    in_weight,
    conv_weight,
    conv_bias,
    proj_weight,
    dt_weight,
    dt_bias,
    a_log,
    skip_gain,
    threshold,
):
    rows, depth = tokens.shape
    width = in_weight.shape[1]
    n_state = a_log.shape[0]
    stride = -(-width // (8 * LANES)) * 8
    groups = stride // 8
    padded = -(-proj_weight.shape[1] // LANES) * LANES
    per = rows // 2 // ntp
    f32, bf16 = jnp.float32, jnp.bfloat16
    sent = bf16 if per % 16 == 0 else f32
    dma = pltpu.SemaphoreType.DMA
    vmem = pl.BlockSpec(memory_space=pltpu.VMEM)
    return pl.pallas_call(
        functools.partial(kernel, ns, ntp),
        out_shape=jax.ShapeDtypeStruct((rows, width), bf16),
        in_specs=[pl.BlockSpec(memory_space=pl.ANY)] * 10,
        out_specs=vmem,
        scratch_shapes=[
            pltpu.VMEM(in_weight.shape, bf16),
            pltpu.VMEM(conv_weight.shape, f32),
            pltpu.VMEM((1, width), f32),
            pltpu.VMEM(proj_weight.shape[::-1], bf16),
            pltpu.VMEM(dt_weight.shape, bf16),
            pltpu.VMEM((1, width), f32),
            pltpu.VMEM(a_log.shape, f32),
            pltpu.VMEM((1, width), f32),
            pltpu.VMEM((1, width), f32),
            pltpu.VMEM((ntp, rows, depth), bf16),
            pltpu.VMEM((rows, width), f32),
            pltpu.VMEM((rows + 8, width), f32),
            pltpu.VMEM((16, width), bf16),
            pltpu.VMEM((16, width), bf16),
            pltpu.VMEM((rows, width), bf16),
            pltpu.VMEM((2, ntp, per, padded), f32),
            pltpu.VMEM((2, ntp, per, padded), sent),
            pltpu.VMEM((2, ntp - 1, per, padded), sent),
            pltpu.VMEM((2, ntp, per, padded), sent),
            pltpu.VMEM((rows, padded), f32),
            pltpu.VMEM((rows * 2 * n_state, LANES), f32),
            pltpu.VMEM((rows * stride, LANES), f32),
            pltpu.VMEM((rows * stride, LANES), f32),
            pltpu.VMEM((rows * stride, LANES), f32),
            pltpu.VMEM((n_state * stride, LANES), f32),
            pltpu.VMEM((groups, n_state * 8 + 8, LANES), f32),
            pltpu.VMEM((groups, n_state * 8 + 16, LANES), bf16),
            pltpu.VMEM((groups, ns - 1, n_state * 8 + 16, LANES), bf16),
            pltpu.VMEM((n_state * 8, LANES), f32),
            dma((ntp,)),
            dma((9,)),
            dma((ntp, 2)),
            dma((ntp, 2)),
            dma((ntp, 2)),
            dma((2,)),
            dma((2, ntp - 1)),
            dma((2, ntp - 1)),
            dma((2, ntp - 1)),
            dma((2, ntp - 1)),
            dma((groups, ns - 1)),
            dma((groups, ns - 1)),
        ],
        compiler_params=pltpu.CompilerParams(
            collective_id=0, has_side_effects=True, vmem_limit_bytes=63 * 1024 * 1024
        ),
    )(
        tokens,
        in_weight,
        conv_weight,
        conv_bias.reshape(1, -1),
        proj_weight.T,
        dt_weight,
        dt_bias.reshape(1, -1),
        a_log,
        skip_gain.reshape(1, -1),
        threshold.reshape(1, -1),
    )


def solution(mesh):
    return jax.shard_map(
        functools.partial(per_device, mesh.shape["seq"], mesh.shape["tp"]),
        mesh=mesh,
        in_specs=(
            P("seq", "tp"),
            P(None, "tp"),
            P(None, "tp"),
            P("tp"),
            P("tp", None),
            P(None, "tp"),
            P("tp"),
            P(None, "tp"),
            P("tp"),
            P("tp"),
        ),
        out_specs=P("seq", "tp"),
        check_vma=False,
    )
```

```python
import functools

import jax
import jax.numpy as jnp
from jax import lax
from jax.experimental import pallas as pl
from jax.experimental.pallas import tpu as pltpu
from jax.sharding import PartitionSpec as P

MESH = pl.DeviceIdType.MESH
LOG2E = 1.4426950408889634
LANES = 128


def kernel(
    ns,
    ntp,
    tok_hbm,
    w_hbm,
    cw_hbm,
    cb_hbm,
    proj_hbm,
    dtw_hbm,
    dtb_hbm,
    alog_hbm,
    skip_hbm,
    thr_hbm,
    out_ref,
    w_ref,
    cw_ref,
    cb_ref,
    proj_ref,
    dtw_ref,
    dtb_ref,
    alog_ref,
    skip_ref,
    thr_ref,
    tok_all,
    acc,
    pad,
    halo_out,
    halo_in,
    u_ref,
    part,
    ps,
    rs,
    ag,
    tot,
    bs,
    dt3,
    du3,
    y3,
    r3,
    later,
    sx,
    sr,
    entry,
    w_sem,
    in_sem,
    tok_recv,
    tok_right,
    tok_left,
    halo_sem,
    rs_send,
    rs_recv,
    ag_send,
    ag_recv,
    st_send,
    st_recv,
):
    q = lax.axis_index("seq")
    z = lax.axis_index("tp")
    rows, depth = tok_hbm.shape
    width = w_ref.shape[1]
    taps = cw_ref.shape[0]
    rank = dtw_ref.shape[0]
    n_state = alog_ref.shape[0]
    cols = proj_ref.shape[0]
    tiles = width // LANES
    stride = r3.shape[0] // n_state
    groups = stride // 8
    per = ag.shape[2]
    f32, bf16 = jnp.float32, jnp.bfloat16
    half = rows // 2
    split = half - 16
    token_rows = ((split, rows - split), (0, split))
    phase_rows = (half, 0)

    small = [
        (cw_hbm, cw_ref),
        (cb_hbm, cb_ref),
        (proj_hbm, proj_ref),
        (dtw_hbm, dtw_ref),
        (dtb_hbm, dtb_ref),
        (alog_hbm, alog_ref),
        (skip_hbm, skip_ref),
        (thr_hbm, thr_ref),
        (tok_hbm, tok_all.at[z]),
    ]

    def in_copy(i):
        return pltpu.make_async_copy(small[i][0], small[i][1], in_sem.at[i])

    def w_copy(k):
        part_k = pl.ds(pl.multiple_of(k * depth, depth), depth)
        return pltpu.make_async_copy(w_hbm.at[part_k], w_ref.at[part_k], w_sem.at[k])

    in_copy(8).start()
    w_copy(z).start()

    barrier = pltpu.get_barrier_semaphore()
    for d in range(1, ntp):
        pl.semaphore_signal(
            barrier, inc=1, device_id={"tp": lax.rem(z + d, ntp)}, device_id_type=MESH
        )
    for d in range(1, ns):
        pl.semaphore_signal(
            barrier, inc=1, device_id={"seq": lax.rem(q + d, ns)}, device_id_type=MESH
        )
    for i in (5, 0, 1, 2, 3, 4, 6, 7):
        in_copy(i).start()
    for i in range(1, ntp):
        w_copy(lax.rem(z + i, ntp)).start()
    pl.semaphore_wait(barrier, ns + ntp - 2)

    def tok_copy(k, h, by, sems, own):
        at = pl.ds(*token_rows[h])
        return pltpu.make_async_remote_copy(
            src_ref=tok_hbm.at[at] if own else tok_all.at[k, at],
            dst_ref=tok_all.at[k, at],
            send_sem=sems.at[k, h],
            recv_sem=tok_recv.at[k, h],
            device_id={"tp": z + by},
            device_id_type=MESH,
        )

    def send_own(h):
        @pl.when(z + 1 < ntp)
        def _():
            tok_copy(z, h, 1, tok_right, True).start()

        @pl.when(z > 0)
        def _():
            tok_copy(z, h, -1, tok_left, True).start()

    def take(d, h):
        @pl.when(z - d >= 0)
        def _():
            tok_copy(z - d, h, 1, tok_right, False).wait_recv()

            @pl.when(z + 1 < ntp)
            def _():
                tok_copy(z - d, h, 1, tok_right, False).start()

        @pl.when(z + d < ntp)
        def _():
            tok_copy(z + d, h, -1, tok_left, False).wait_recv()

            @pl.when(z > 0)
            def _():
                tok_copy(z + d, h, -1, tok_left, False).start()

    tn = min(512, width)

    def multiply(k, h, first):
        if h == 0:
            w_copy(k).wait()
        part_k = pl.ds(pl.multiple_of(k * depth, depth), depth)
        mine = pl.ds(*token_rows[h])

        @pl.loop(0, width // tn)
        def _(i):
            at = pl.ds(pl.multiple_of(i * tn, tn), tn)
            got = jnp.dot(tok_all[k, mine, :], w_ref[part_k, at], preferred_element_type=f32)
            acc[mine, at] = got if first else acc[mine, at] + got

    def multiply_pair(d, h):
        @pl.when(z - d >= 0)
        def _():
            multiply(z - d, h, False)

        @pl.when(z + d < ntp)
        def _():
            multiply(z + d, h, False)

    halo = pltpu.make_async_remote_copy(
        src_ref=halo_out,
        dst_ref=halo_in,
        send_sem=halo_sem.at[0],
        recv_sem=halo_sem.at[1],
        device_id={"seq": q + 1},
        device_id_type=MESH,
    )

    def rs_copy(p, d):
        to = lax.rem(z + d, ntp)
        return pltpu.make_async_remote_copy(
            src_ref=ps.at[p, to],
            dst_ref=rs.at[p, d - 1],
            send_sem=rs_send.at[p, d - 1],
            recv_sem=rs_recv.at[p, d - 1],
            device_id={"tp": to},
            device_id_type=MESH,
        )

    def ag_copy(p, d):
        to = lax.rem(z + d, ntp)
        return pltpu.make_async_remote_copy(
            src_ref=ag.at[p, z],
            dst_ref=ag.at[p, z],
            send_sem=ag_send.at[p, d - 1],
            recv_sem=ag_recv.at[p, d - 1],
            device_id={"tp": to},
            device_id_type=MESH,
        )

    def project(p):
        r0 = phase_rows[p]
        for j in range(tiles):
            at = slice(j * LANES, (j + 1) * LANES)
            pre = cb_ref[:, at] + cw_ref[0:1, at] * pad[pl.ds(r0 + 9 - taps, half), at]
            for k in range(1, taps):
                pre = pre + cw_ref[k : k + 1, at] * pad[pl.ds(r0 + 9 - taps + k, half), at]
            u_ref[pl.ds(r0, half), at] = (pre / (1.0 + jnp.exp(-pre))).astype(bf16)
        sums = lax.dot_general(
            u_ref[pl.ds(r0, half), :],
            proj_ref[...],
            (((1,), (1,)), ((), ())),
            preferred_element_type=f32,
        )
        for k in range(ntp):
            mine = sums[k * per : (k + 1) * per]
            part[p, k, :, :cols] = mine
            ps[p, k, :, :cols] = mine.astype(ps.dtype)
        for d in range(1, ntp):
            rs_copy(p, d).start()

    def reduce(p):
        red = part[p, z]
        for d in range(1, ntp):
            rs_copy(p, d).wait_recv()
            red = red + rs[p, d - 1].astype(f32)
        ag[p, z] = red.astype(ag.dtype)
        for d in range(1, ntp):
            ag_copy(p, d).start()

    two = 2 * n_state

    def prepare(p):
        r0 = phase_rows[p]
        mine = pl.ds(r0, half)
        for d in range(1, ntp):
            ag_copy(p, d).wait_recv()
        for k in range(ntp):
            tot[pl.ds(r0 + k * per, per), :] = ag[p, k].astype(f32)
        dt_low = tot[mine, :rank].astype(bf16)
        for j0 in range(0, width, tn):
            at = slice(j0, j0 + tn)
            v = jnp.dot(dt_low, dtw_ref[:, at], preferred_element_type=f32) + dtb_ref[:, at]
            v = jnp.maximum(v, 0.0) + jnp.log1p(jnp.exp(-jnp.abs(v)))
            flow = v * u_ref[mine, at].astype(f32)
            for i in range(tn // LANES):
                cut = slice(i * LANES, (i + 1) * LANES)
                to = pl.ds(r0 * stride + j0 // LANES + i, half, stride=stride)
                dt3[to, :] = v[:, cut]
                du3[to, :] = flow[:, cut]
        for n in range(two):
            bs[pl.ds(r0 * two + n, half, stride=two), :] = jnp.broadcast_to(
                tot[mine, rank + n : rank + n + 1], (half, LANES)
            )

    def rates(g):
        return [r3[pl.ds(n * stride + g * 8, 8), :] for n in range(n_state)]

    def splat(t, n):
        return bs[pl.ds(t * two + n, 8, stride=0), :]

    def st_copy(g, d):
        return pltpu.make_async_remote_copy(
            src_ref=sx.at[g],
            dst_ref=sr.at[g, d - 1],
            send_sem=st_send.at[g, d - 1],
            recv_sem=st_recv.at[g, d - 1],
            device_id={"seq": q + d},
            device_id_type=MESH,
        )

    def first_pass(p, g):
        rate = rates(g)
        r0 = phase_rows[p]

        def step(t, carry):
            states, total = carry
            at = pl.ds(pl.multiple_of(t * stride + g * 8, 8), 8)
            dt, du = dt3[at, :], du3[at, :]
            states = [
                jnp.exp2(dt * rate[n]) * states[n] + du * splat(t, n) for n in range(n_state)
            ]
            return states, total + dt

        zero = jnp.zeros((8, LANES), f32)
        states, total = lax.fori_loop(
            r0, r0 + half, step, ([zero] * n_state, zero), unroll=16
        )
        if p == 0:
            for n in range(n_state):
                later[g, pl.ds(n * 8, 8), :] = states[n]
            later[g, pl.ds(n_state * 8, 8), :] = total
            return
        more = later[g, pl.ds(n_state * 8, 8), :]
        states = [
            jnp.exp2(more * rate[n]) * states[n] + later[g, pl.ds(n * 8, 8), :]
            for n in range(n_state)
        ]
        total = total + more
        high = total.astype(bf16).astype(f32)
        items = states + [high, total - high]
        for n in range(0, len(items), 2):
            sx[g, pl.ds(n * 8, 16), :] = jnp.concatenate(items[n : n + 2], axis=0).astype(bf16)
        for d in range(1, ns):

            @pl.when(q + d < ns)
            def _():
                st_copy(g, d).start()

    def second_pass(g):
        rate = rates(g)
        zero = jnp.zeros((8, LANES), f32)
        for n in range(n_state):
            entry[pl.ds(n * 8, 8), :] = zero
        for d in range(ns - 1, 0, -1):

            @pl.when(q - d >= 0)
            def _():
                st_copy(g, d).wait_recv()
                sums = sr[g, d - 1, pl.ds(n_state * 8, 16), :].astype(f32)
                sums = sums[:8] + sums[8:]
                for n in range(0, n_state, 2):
                    ends = sr[g, d - 1, pl.ds(n * 8, 16), :].astype(f32)
                    for i in range(2):
                        at = pl.ds((n + i) * 8, 8)
                        entry[at, :] = (
                            jnp.exp2(sums * rate[n + i]) * entry[at, :] + ends[i * 8 : i * 8 + 8]
                        )

        def step(t, states):
            at = pl.ds(pl.multiple_of(t * stride + g * 8, 8), 8)
            dt, du = dt3[at, :], du3[at, :]
            states = [
                jnp.exp2(dt * rate[n]) * states[n] + du * splat(t, n) for n in range(n_state)
            ]
            terms = [splat(t, n_state + n) * states[n] for n in range(n_state)]
            while len(terms) > 1:
                terms = [a + b for a, b in zip(terms[::2], terms[1::2])]
            y3[at, :] = terms[0]
            return states

        lax.fori_loop(0, rows, step, [entry[pl.ds(n * 8, 8), :] for n in range(n_state)], unroll=16)
        for j in range(g * 8, min(g * 8 + 8, tiles)):
            at = slice(j * LANES, (j + 1) * LANES)
            y = y3[pl.ds(j, rows, stride=stride), :] + skip_ref[:, at] * u_ref[:, at].astype(f32)
            out_ref[:, at] = (y / (1.0 + jnp.exp(-4.0 * (y - thr_ref[:, at])))).astype(bf16)

    send_own(0)
    in_copy(8).wait()
    in_copy(5).wait()
    for j in range(tiles):
        at = slice(j * LANES, (j + 1) * LANES)
        r3[pl.ds(j, n_state, stride=stride), :] = -LOG2E * jnp.exp(alog_ref[:, at])
    part[:, :, :, cols:] = jnp.zeros(part.shape[:3] + (part.shape[3] - cols,), f32)
    ps[:, :, :, cols:] = jnp.zeros(ps.shape[:3] + (ps.shape[3] - cols,), ps.dtype)
    send_own(1)
    multiply(z, 0, True)
    for d in range(1, ntp):
        take(d, 0)
        multiply_pair(d, 0)
        if d < ntp - 1:
            take(d, 1)
    halo_out[...] = acc[rows - 16 :, :].astype(bf16)

    @pl.when(q + 1 < ns)
    def _():
        halo.start()

    pad[pl.ds(8 + split, rows - split), :] = acc[split:, :].astype(bf16).astype(f32)
    for i in (0, 1, 2):
        in_copy(i).wait()
    project(0)

    multiply(z, 1, True)
    for d in range(1, ntp - 1):
        multiply_pair(d, 1)
    reduce(0)
    if ntp > 1:
        take(ntp - 1, 1)
        multiply_pair(ntp - 1, 1)
    pad[pl.ds(8, split), :] = acc[:split, :].astype(bf16).astype(f32)

    @pl.when(q > 0)
    def _():
        halo.wait_recv()
        pad[pl.ds(0, 8), :] = halo_in[...].astype(f32)[8:]

    @pl.when(q == 0)
    def _():
        pad[pl.ds(0, 8), :] = jnp.zeros((8, width), f32)

    project(1)

    in_copy(3).wait()
    in_copy(4).wait()
    prepare(0)
    reduce(1)
    for g in range(groups):
        first_pass(0, g)
    prepare(1)
    for g in range(groups):
        first_pass(1, g)
    in_copy(6).wait()
    in_copy(7).wait()
    for g in range(groups):
        second_pass(g)

    for k in range(ntp):
        for h in range(2):

            @pl.when((z + 1 < ntp) & (k <= z))
            def _():
                tok_copy(k, h, 1, tok_right, False).wait_send()

            @pl.when((z > 0) & (k >= z))
            def _():
                tok_copy(k, h, -1, tok_left, False).wait_send()

    @pl.when(q + 1 < ns)
    def _():
        halo.wait_send()

    for p in range(2):
        for d in range(1, ntp):
            rs_copy(p, d).wait_send()
            ag_copy(p, d).wait_send()
    for g in range(groups):
        for d in range(1, ns):

            @pl.when(q + d < ns)
            def _():
                st_copy(g, d).wait_send()


def per_device(
    ns,
    ntp,
    tokens,
    in_weight,
    conv_weight,
    conv_bias,
    proj_weight,
    dt_weight,
    dt_bias,
    a_log,
    skip_gain,
    threshold,
):
    rows, depth = tokens.shape
    width = in_weight.shape[1]
    n_state = a_log.shape[0]
    stride = -(-width // (8 * LANES)) * 8
    groups = stride // 8
    padded = -(-proj_weight.shape[1] // LANES) * LANES
    per = rows // 2 // ntp
    f32, bf16 = jnp.float32, jnp.bfloat16
    sent = bf16 if per % 16 == 0 else f32
    dma = pltpu.SemaphoreType.DMA
    vmem = pl.BlockSpec(memory_space=pltpu.VMEM)
    return pl.pallas_call(
        functools.partial(kernel, ns, ntp),
        out_shape=jax.ShapeDtypeStruct((rows, width), bf16),
        in_specs=[pl.BlockSpec(memory_space=pl.ANY)] * 10,
        out_specs=vmem,
        scratch_shapes=[
            pltpu.VMEM(in_weight.shape, bf16),
            pltpu.VMEM(conv_weight.shape, f32),
            pltpu.VMEM((1, width), f32),
            pltpu.VMEM(proj_weight.shape[::-1], bf16),
            pltpu.VMEM(dt_weight.shape, bf16),
            pltpu.VMEM((1, width), f32),
            pltpu.VMEM(a_log.shape, f32),
            pltpu.VMEM((1, width), f32),
            pltpu.VMEM((1, width), f32),
            pltpu.VMEM((ntp, rows, depth), bf16),
            pltpu.VMEM((rows, width), f32),
            pltpu.VMEM((rows + 8, width), f32),
            pltpu.VMEM((16, width), bf16),
            pltpu.VMEM((16, width), bf16),
            pltpu.VMEM((rows, width), bf16),
            pltpu.VMEM((2, ntp, per, padded), f32),
            pltpu.VMEM((2, ntp, per, padded), sent),
            pltpu.VMEM((2, ntp - 1, per, padded), sent),
            pltpu.VMEM((2, ntp, per, padded), sent),
            pltpu.VMEM((rows, padded), f32),
            pltpu.VMEM((rows * 2 * n_state + 8, LANES), f32),
            pltpu.VMEM((rows * stride, LANES), f32),
            pltpu.VMEM((rows * stride, LANES), f32),
            pltpu.VMEM((rows * stride, LANES), f32),
            pltpu.VMEM((n_state * stride, LANES), f32),
            pltpu.VMEM((groups, n_state * 8 + 8, LANES), f32),
            pltpu.VMEM((groups, n_state * 8 + 16, LANES), bf16),
            pltpu.VMEM((groups, ns - 1, n_state * 8 + 16, LANES), bf16),
            pltpu.VMEM((n_state * 8, LANES), f32),
            dma((ntp,)),
            dma((9,)),
            dma((ntp, 2)),
            dma((ntp, 2)),
            dma((ntp, 2)),
            dma((2,)),
            dma((2, ntp - 1)),
            dma((2, ntp - 1)),
            dma((2, ntp - 1)),
            dma((2, ntp - 1)),
            dma((groups, ns - 1)),
            dma((groups, ns - 1)),
        ],
        compiler_params=pltpu.CompilerParams(
            collective_id=0, has_side_effects=True, vmem_limit_bytes=63 * 1024 * 1024
        ),
    )(
        tokens,
        in_weight,
        conv_weight,
        conv_bias.reshape(1, -1),
        proj_weight.T,
        dt_weight,
        dt_bias.reshape(1, -1),
        a_log,
        skip_gain.reshape(1, -1),
        threshold.reshape(1, -1),
    )


def solution(mesh):
    return jax.shard_map(
        functools.partial(per_device, mesh.shape["seq"], mesh.shape["tp"]),
        mesh=mesh,
        in_specs=(
            P("seq", "tp"),
            P(None, "tp"),
            P(None, "tp"),
            P("tp"),
            P("tp", None),
            P(None, "tp"),
            P("tp"),
            P(None, "tp"),
            P("tp"),
            P("tp"),
        ),
        out_specs=P("seq", "tp"),
        check_vma=False,
    )
```

```python
import functools

import jax
import jax.numpy as jnp
from jax import lax
from jax.experimental import pallas as pl
from jax.experimental.pallas import tpu as pltpu
from jax.sharding import PartitionSpec as P

MESH = pl.DeviceIdType.MESH
LOG2E = 1.4426950408889634
LANES = 128


def kernel(
    ns,
    ntp,
    tok_hbm,
    w_hbm,
    cw_hbm,
    cb_hbm,
    proj_hbm,
    dtw_hbm,
    dtb_hbm,
    alog_hbm,
    skip_hbm,
    thr_hbm,
    out_ref,
    w_ref,
    cw_ref,
    cb_ref,
    proj_ref,
    dtw_ref,
    dtb_ref,
    alog_ref,
    skip_ref,
    thr_ref,
    tok_all,
    acc,
    pad,
    halo_out,
    halo_in,
    u_ref,
    part,
    ps,
    rs,
    ag,
    tot,
    bs,
    dt3,
    du3,
    y3,
    r3,
    later,
    sx,
    sr,
    entry,
    w_sem,
    in_sem,
    tok_recv,
    tok_right,
    tok_left,
    halo_sem,
    rs_send,
    rs_recv,
    ag_send,
    ag_recv,
    st_send,
    st_recv,
):
    q = lax.axis_index("seq")
    z = lax.axis_index("tp")
    rows, depth = tok_hbm.shape
    width = w_ref.shape[1]
    taps = cw_ref.shape[0]
    rank = dtw_ref.shape[0]
    n_state = alog_ref.shape[0]
    cols = proj_ref.shape[0]
    tiles = width // LANES
    stride = r3.shape[0] // n_state
    groups = stride // 8
    per = ag.shape[2]
    f32, bf16 = jnp.float32, jnp.bfloat16
    half = rows // 2
    split = half - 16
    token_rows = ((split, rows - split), (0, split))
    phase_rows = (half, 0)

    small = [
        (cw_hbm, cw_ref),
        (cb_hbm, cb_ref),
        (proj_hbm, proj_ref),
        (dtw_hbm, dtw_ref),
        (dtb_hbm, dtb_ref),
        (alog_hbm, alog_ref),
        (skip_hbm, skip_ref),
        (thr_hbm, thr_ref),
        (tok_hbm, tok_all.at[z]),
    ]

    def tile_at(j):
        return pl.ds(pl.multiple_of(j * LANES, LANES), LANES)

    def sigmoid(v):
        return 0.5 + 0.5 * jnp.tanh(0.5 * v)

    def in_copy(i):
        return pltpu.make_async_copy(small[i][0], small[i][1], in_sem.at[i])

    def w_copy(k):
        part_k = pl.ds(pl.multiple_of(k * depth, depth), depth)
        return pltpu.make_async_copy(w_hbm.at[part_k], w_ref.at[part_k], w_sem.at[k])

    in_copy(8).start()
    w_copy(z).start()

    barrier = pltpu.get_barrier_semaphore()
    for d in range(1, ntp):
        pl.semaphore_signal(
            barrier, inc=1, device_id={"tp": lax.rem(z + d, ntp)}, device_id_type=MESH
        )
    for d in range(1, ns):
        pl.semaphore_signal(
            barrier, inc=1, device_id={"seq": lax.rem(q + d, ns)}, device_id_type=MESH
        )
    for i in (5, 0, 1, 2, 3, 4, 6, 7):
        in_copy(i).start()
    for i in range(1, ntp):
        w_copy(lax.rem(z + i, ntp)).start()
    pl.semaphore_wait(barrier, ns + ntp - 2)

    def tok_copy(k, h, by, sems, own):
        at = pl.ds(*token_rows[h])
        return pltpu.make_async_remote_copy(
            src_ref=tok_hbm.at[at] if own else tok_all.at[k, at],
            dst_ref=tok_all.at[k, at],
            send_sem=sems.at[k, h],
            recv_sem=tok_recv.at[k, h],
            device_id={"tp": z + by},
            device_id_type=MESH,
        )

    def send_own(h):
        @pl.when(z + 1 < ntp)
        def _():
            tok_copy(z, h, 1, tok_right, True).start()

        @pl.when(z > 0)
        def _():
            tok_copy(z, h, -1, tok_left, True).start()

    def take(d, h):
        @pl.when(z - d >= 0)
        def _():
            tok_copy(z - d, h, 1, tok_right, False).wait_recv()

            @pl.when(z + 1 < ntp)
            def _():
                tok_copy(z - d, h, 1, tok_right, False).start()

        @pl.when(z + d < ntp)
        def _():
            tok_copy(z + d, h, -1, tok_left, False).wait_recv()

            @pl.when(z > 0)
            def _():
                tok_copy(z + d, h, -1, tok_left, False).start()

    tn = min(512, width)

    def multiply(k, h, first):
        if h == 0:
            w_copy(k).wait()
        part_k = pl.ds(pl.multiple_of(k * depth, depth), depth)
        mine = pl.ds(*token_rows[h])

        @pl.loop(0, width // tn)
        def _(i):
            at = pl.ds(pl.multiple_of(i * tn, tn), tn)
            got = jnp.dot(tok_all[k, mine, :], w_ref[part_k, at], preferred_element_type=f32)
            acc[mine, at] = got if first else acc[mine, at] + got

    def multiply_pair(d, h):
        @pl.when(z - d >= 0)
        def _():
            multiply(z - d, h, False)

        @pl.when(z + d < ntp)
        def _():
            multiply(z + d, h, False)

    halo = pltpu.make_async_remote_copy(
        src_ref=halo_out,
        dst_ref=halo_in,
        send_sem=halo_sem.at[0],
        recv_sem=halo_sem.at[1],
        device_id={"seq": q + 1},
        device_id_type=MESH,
    )

    def rs_copy(p, d):
        to = lax.rem(z + d, ntp)
        return pltpu.make_async_remote_copy(
            src_ref=ps.at[p, to],
            dst_ref=rs.at[p, d - 1],
            send_sem=rs_send.at[p, d - 1],
            recv_sem=rs_recv.at[p, d - 1],
            device_id={"tp": to},
            device_id_type=MESH,
        )

    def ag_copy(p, d):
        to = lax.rem(z + d, ntp)
        return pltpu.make_async_remote_copy(
            src_ref=ag.at[p, z],
            dst_ref=ag.at[p, z],
            send_sem=ag_send.at[p, d - 1],
            recv_sem=ag_recv.at[p, d - 1],
            device_id={"tp": to},
            device_id_type=MESH,
        )

    def project(p):
        r0 = phase_rows[p]

        @pl.loop(0, tiles)
        def _(j):
            at = tile_at(j)
            pre = cb_ref[:, at] + cw_ref[0:1, at] * pad[pl.ds(r0 + 9 - taps, half), at]
            for k in range(1, taps):
                pre = pre + cw_ref[k : k + 1, at] * pad[pl.ds(r0 + 9 - taps + k, half), at]
            u_ref[pl.ds(r0, half), at] = (pre * sigmoid(pre)).astype(bf16)

        sums = lax.dot_general(
            u_ref[pl.ds(r0, half), :],
            proj_ref[...],
            (((1,), (1,)), ((), ())),
            preferred_element_type=f32,
        )
        for k in range(ntp):
            mine = sums[k * per : (k + 1) * per]
            part[p, k, :, :cols] = mine
            ps[p, k, :, :cols] = mine.astype(ps.dtype)
        for d in range(1, ntp):
            rs_copy(p, d).start()

    def reduce(p):
        red = part[p, z]
        for d in range(1, ntp):
            rs_copy(p, d).wait_recv()
            red = red + rs[p, d - 1].astype(f32)
        ag[p, z] = red.astype(ag.dtype)
        for d in range(1, ntp):
            ag_copy(p, d).start()

    two = 2 * n_state

    def prepare(p):
        r0 = phase_rows[p]
        mine = pl.ds(r0, half)
        for d in range(1, ntp):
            ag_copy(p, d).wait_recv()
        for k in range(ntp):
            tot[pl.ds(r0 + k * per, per), :] = ag[p, k].astype(f32)
        dt_low = tot[mine, :rank].astype(bf16)

        @pl.loop(0, width // tn)
        def _(s):
            at = pl.ds(pl.multiple_of(s * tn, tn), tn)
            v = jnp.dot(dt_low, dtw_ref[:, at], preferred_element_type=f32) + dtb_ref[:, at]
            e = jnp.exp(-jnp.abs(v))
            e = jnp.where(e < 1e-3, e - (0.5 * e) * e, jnp.log(1.0 + e))
            v = jnp.maximum(v, 0.0) + e
            flow = v * u_ref[mine, at].astype(f32)
            for i in range(tn // LANES):
                cut = slice(i * LANES, (i + 1) * LANES)
                to = pl.ds(r0 * stride + s * (tn // LANES) + i, half, stride=stride)
                dt3[to, :] = v[:, cut]
                du3[to, :] = flow[:, cut]

        for n in range(two):
            bs[pl.ds(n * rows + r0, half), :] = jnp.broadcast_to(
                tot[mine, rank + n : rank + n + 1], (half, LANES)
            )

    def rates(g):
        return [
            r3[pl.ds(pl.multiple_of(n * stride + g * 8, 8), 8), :] for n in range(n_state)
        ]

    def splat(t, n):
        return bs[pl.ds(n * rows + t, 8, stride=0), :]

    def st_copy(g, d):
        return pltpu.make_async_remote_copy(
            src_ref=sx.at[g],
            dst_ref=sr.at[g, d - 1],
            send_sem=st_send.at[g, d - 1],
            recv_sem=st_recv.at[g, d - 1],
            device_id={"seq": q + d},
            device_id_type=MESH,
        )

    def first_pass(p, g):
        rate = rates(g)
        r0 = phase_rows[p]

        def step(t, carry):
            states, total = carry
            at = pl.ds(pl.multiple_of(t * stride + g * 8, 8), 8)
            dt, du = dt3[at, :], du3[at, :]
            states = [
                jnp.exp2(dt * rate[n]) * states[n] + du * splat(t, n) for n in range(n_state)
            ]
            return states, total + dt

        zero = jnp.zeros((8, LANES), f32)
        states, total = lax.fori_loop(
            r0, r0 + half, step, ([zero] * n_state, zero), unroll=8
        )
        if p == 0:
            for n in range(n_state):
                later[g, pl.ds(n * 8, 8), :] = states[n]
            later[g, pl.ds(n_state * 8, 8), :] = total
            return
        more = later[g, pl.ds(n_state * 8, 8), :]
        states = [
            jnp.exp2(more * rate[n]) * states[n] + later[g, pl.ds(n * 8, 8), :]
            for n in range(n_state)
        ]
        total = total + more
        high = total.astype(bf16).astype(f32)
        items = states + [high, total - high]
        for n in range(0, len(items), 2):
            sx[g, pl.ds(n * 8, 16), :] = jnp.concatenate(items[n : n + 2], axis=0).astype(bf16)
        for d in range(1, ns):

            @pl.when(q + d < ns)
            def _():
                st_copy(g, d).start()

    def second_pass(g):
        rate = rates(g)
        zero = jnp.zeros((8, LANES), f32)
        for n in range(n_state):
            entry[pl.ds(n * 8, 8), :] = zero
        for d in range(ns - 1, 0, -1):

            @pl.when(q - d >= 0)
            def _():
                st_copy(g, d).wait_recv()
                sums = sr[g, d - 1, pl.ds(n_state * 8, 16), :].astype(f32)
                sums = sums[:8] + sums[8:]
                for n in range(0, n_state, 2):
                    ends = sr[g, d - 1, pl.ds(n * 8, 16), :].astype(f32)
                    for i in range(2):
                        at = pl.ds((n + i) * 8, 8)
                        entry[at, :] = (
                            jnp.exp2(sums * rate[n + i]) * entry[at, :] + ends[i * 8 : i * 8 + 8]
                        )

        def step(t, states):
            at = pl.ds(pl.multiple_of(t * stride + g * 8, 8), 8)
            dt, du = dt3[at, :], du3[at, :]
            states = [
                jnp.exp2(dt * rate[n]) * states[n] + du * splat(t, n) for n in range(n_state)
            ]
            terms = [splat(t, n_state + n) * states[n] for n in range(n_state)]
            while len(terms) > 1:
                terms = [a + b for a, b in zip(terms[::2], terms[1::2])]
            y3[at, :] = terms[0]
            return states

        lax.fori_loop(0, rows, step, [entry[pl.ds(n * 8, 8), :] for n in range(n_state)], unroll=8)

        @pl.loop(g * 8, jnp.minimum(g * 8 + 8, tiles))
        def _(j):
            at = tile_at(j)
            y = y3[pl.ds(j, rows, stride=stride), :] + skip_ref[:, at] * u_ref[:, at].astype(f32)
            out_ref[:, at] = (y * sigmoid(4.0 * (y - thr_ref[:, at]))).astype(bf16)

    send_own(0)
    in_copy(8).wait()
    in_copy(5).wait()
    for j in range(tiles):
        at = slice(j * LANES, (j + 1) * LANES)
        r3[pl.ds(j, n_state, stride=stride), :] = -LOG2E * jnp.exp(alog_ref[:, at])
    part[:, :, :, cols:] = jnp.zeros(part.shape[:3] + (part.shape[3] - cols,), f32)
    ps[:, :, :, cols:] = jnp.zeros(ps.shape[:3] + (ps.shape[3] - cols,), ps.dtype)
    send_own(1)
    multiply(z, 0, True)

    @pl.loop(1, ntp)
    def _(d):
        take(d, 0)
        multiply_pair(d, 0)

        @pl.when(d < ntp - 1)
        def _():
            take(d, 1)

    halo_out[...] = acc[rows - 16 :, :].astype(bf16)

    @pl.when(q + 1 < ns)
    def _():
        halo.start()

    pad[pl.ds(8 + split, rows - split), :] = acc[split:, :].astype(bf16).astype(f32)
    for i in (0, 1, 2):
        in_copy(i).wait()
    project(0)

    multiply(z, 1, True)

    @pl.loop(1, ntp - 1)
    def _(d):
        multiply_pair(d, 1)

    reduce(0)
    if ntp > 1:
        take(ntp - 1, 1)
        multiply_pair(ntp - 1, 1)
    pad[pl.ds(8, split), :] = acc[:split, :].astype(bf16).astype(f32)

    @pl.when(q > 0)
    def _():
        halo.wait_recv()
        pad[pl.ds(0, 8), :] = halo_in[...].astype(f32)[8:]

    @pl.when(q == 0)
    def _():
        pad[pl.ds(0, 8), :] = jnp.zeros((8, width), f32)

    project(1)

    in_copy(3).wait()
    in_copy(4).wait()
    prepare(0)
    reduce(1)

    @pl.loop(0, groups)
    def _(g):
        first_pass(0, g)

    prepare(1)

    @pl.loop(0, groups)
    def _(g):
        first_pass(1, g)

    in_copy(6).wait()
    in_copy(7).wait()

    @pl.loop(0, groups)
    def _(g):
        second_pass(g)


    for k in range(ntp):
        for h in range(2):

            @pl.when((z + 1 < ntp) & (k <= z))
            def _():
                tok_copy(k, h, 1, tok_right, False).wait_send()

            @pl.when((z > 0) & (k >= z))
            def _():
                tok_copy(k, h, -1, tok_left, False).wait_send()

    @pl.when(q + 1 < ns)
    def _():
        halo.wait_send()

    for p in range(2):
        for d in range(1, ntp):
            rs_copy(p, d).wait_send()
            ag_copy(p, d).wait_send()
    for g in range(groups):
        for d in range(1, ns):

            @pl.when(q + d < ns)
            def _():
                st_copy(g, d).wait_send()


def per_device(
    ns,
    ntp,
    tokens,
    in_weight,
    conv_weight,
    conv_bias,
    proj_weight,
    dt_weight,
    dt_bias,
    a_log,
    skip_gain,
    threshold,
):
    rows, depth = tokens.shape
    width = in_weight.shape[1]
    n_state = a_log.shape[0]
    stride = -(-width // (8 * LANES)) * 8
    groups = stride // 8
    padded = -(-proj_weight.shape[1] // LANES) * LANES
    per = rows // 2 // ntp
    f32, bf16 = jnp.float32, jnp.bfloat16
    sent = bf16 if per % 16 == 0 else f32
    dma = pltpu.SemaphoreType.DMA
    vmem = pl.BlockSpec(memory_space=pltpu.VMEM)
    return pl.pallas_call(
        functools.partial(kernel, ns, ntp),
        out_shape=jax.ShapeDtypeStruct((rows, width), bf16),
        in_specs=[pl.BlockSpec(memory_space=pl.ANY)] * 10,
        out_specs=vmem,
        scratch_shapes=[
            pltpu.VMEM(in_weight.shape, bf16),
            pltpu.VMEM(conv_weight.shape, f32),
            pltpu.VMEM((1, width), f32),
            pltpu.VMEM(proj_weight.shape[::-1], bf16),
            pltpu.VMEM(dt_weight.shape, bf16),
            pltpu.VMEM((1, width), f32),
            pltpu.VMEM(a_log.shape, f32),
            pltpu.VMEM((1, width), f32),
            pltpu.VMEM((1, width), f32),
            pltpu.VMEM((ntp, rows, depth), bf16),
            pltpu.VMEM((rows, width), f32),
            pltpu.VMEM((rows + 8, width), f32),
            pltpu.VMEM((16, width), bf16),
            pltpu.VMEM((16, width), bf16),
            pltpu.VMEM((rows, width), bf16),
            pltpu.VMEM((2, ntp, per, padded), f32),
            pltpu.VMEM((2, ntp, per, padded), sent),
            pltpu.VMEM((2, ntp - 1, per, padded), sent),
            pltpu.VMEM((2, ntp, per, padded), sent),
            pltpu.VMEM((rows, padded), f32),
            pltpu.VMEM((rows * 2 * n_state + 8, LANES), f32),
            pltpu.VMEM((rows * stride, LANES), f32),
            pltpu.VMEM((rows * stride, LANES), f32),
            pltpu.VMEM((rows * stride, LANES), f32),
            pltpu.VMEM((n_state * stride, LANES), f32),
            pltpu.VMEM((groups, n_state * 8 + 8, LANES), f32),
            pltpu.VMEM((groups, n_state * 8 + 16, LANES), bf16),
            pltpu.VMEM((groups, ns - 1, n_state * 8 + 16, LANES), bf16),
            pltpu.VMEM((n_state * 8, LANES), f32),
            dma((ntp,)),
            dma((9,)),
            dma((ntp, 2)),
            dma((ntp, 2)),
            dma((ntp, 2)),
            dma((2,)),
            dma((2, ntp - 1)),
            dma((2, ntp - 1)),
            dma((2, ntp - 1)),
            dma((2, ntp - 1)),
            dma((groups, ns - 1)),
            dma((groups, ns - 1)),
        ],
        compiler_params=pltpu.CompilerParams(
            collective_id=0, has_side_effects=True, vmem_limit_bytes=63 * 1024 * 1024
        ),
    )(
        tokens,
        in_weight,
        conv_weight,
        conv_bias.reshape(1, -1),
        proj_weight.T,
        dt_weight,
        dt_bias.reshape(1, -1),
        a_log,
        skip_gain.reshape(1, -1),
        threshold.reshape(1, -1),
    )


def solution(mesh):
    return jax.shard_map(
        functools.partial(per_device, mesh.shape["seq"], mesh.shape["tp"]),
        mesh=mesh,
        in_specs=(
            P("seq", "tp"),
            P(None, "tp"),
            P(None, "tp"),
            P("tp"),
            P("tp", None),
            P(None, "tp"),
            P("tp"),
            P(None, "tp"),
            P("tp"),
            P("tp"),
        ),
        out_specs=P("seq", "tp"),
        check_vma=False,
    )
```

```python
import functools

import jax
import jax.numpy as jnp
from jax import lax
from jax.experimental import pallas as pl
from jax.experimental.pallas import tpu as pltpu
from jax.sharding import PartitionSpec as P

MESH = pl.DeviceIdType.MESH
LOG2E = 1.4426950408889634
LANES = 128
PIECES = 4


def kernel(
    ns,
    ntp,
    tok_hbm,
    w_hbm,
    cw_hbm,
    cb_hbm,
    proj_hbm,
    dtw_hbm,
    dtb_hbm,
    alog_hbm,
    skip_hbm,
    thr_hbm,
    out_ref,
    w_ref,
    cw_ref,
    cb_ref,
    proj_ref,
    dtw_ref,
    dtb_ref,
    alog_ref,
    skip_ref,
    thr_ref,
    tok_all,
    acc,
    pad,
    halo_out,
    halo_in,
    u_ref,
    part,
    ps,
    rs,
    ag,
    tot,
    bs,
    dt3,
    du3,
    y3,
    r3,
    later,
    sx,
    sr,
    entry,
    w_sem,
    in_sem,
    tok_recv,
    tok_right,
    tok_left,
    halo_sem,
    rs_send,
    rs_recv,
    ag_send,
    ag_recv,
    st_send,
    st_recv,
):
    q = lax.axis_index("seq")
    z = lax.axis_index("tp")
    rows, depth = tok_hbm.shape
    width = w_ref.shape[1]
    taps = cw_ref.shape[0]
    rank = dtw_ref.shape[0]
    n_state = alog_ref.shape[0]
    cols = proj_ref.shape[0]
    tiles = width // LANES
    stride = r3.shape[0] // n_state
    groups = stride // 8
    per = ag.shape[2]
    f32, bf16 = jnp.float32, jnp.bfloat16
    half = rows // 2
    piece = rows // PIECES
    phase_rows = (half, 0)

    small = [
        (cw_hbm, cw_ref),
        (cb_hbm, cb_ref),
        (proj_hbm, proj_ref),
        (dtw_hbm, dtw_ref),
        (dtb_hbm, dtb_ref),
        (alog_hbm, alog_ref),
        (skip_hbm, skip_ref),
        (thr_hbm, thr_ref),
        (tok_hbm, tok_all.at[z]),
    ]

    def tile_at(j):
        return pl.ds(pl.multiple_of(j * LANES, LANES), LANES)

    def sigmoid(v):
        return 0.5 + 0.5 * jnp.tanh(0.5 * v)

    def in_copy(i):
        return pltpu.make_async_copy(small[i][0], small[i][1], in_sem.at[i])

    def w_copy(k):
        part_k = pl.ds(pl.multiple_of(k * depth, depth), depth)
        return pltpu.make_async_copy(w_hbm.at[part_k], w_ref.at[part_k], w_sem.at[k])

    in_copy(8).start()
    w_copy(z).start()

    barrier = pltpu.get_barrier_semaphore()
    for d in range(1, ntp):
        pl.semaphore_signal(
            barrier, inc=1, device_id={"tp": lax.rem(z + d, ntp)}, device_id_type=MESH
        )
    for d in range(1, ns):
        pl.semaphore_signal(
            barrier, inc=1, device_id={"seq": lax.rem(q + d, ns)}, device_id_type=MESH
        )
    for i in (5, 0, 1, 2, 3, 4, 6, 7):
        in_copy(i).start()
    for i in range(1, ntp):
        w_copy(lax.rem(z + i, ntp)).start()
    pl.semaphore_wait(barrier, ns + ntp - 2)

    def tok_copy(k, h, by, sems, own):
        at = pl.ds(h * piece, piece)
        return pltpu.make_async_remote_copy(
            src_ref=tok_hbm.at[at] if own else tok_all.at[k, at],
            dst_ref=tok_all.at[k, at],
            send_sem=sems.at[k, h],
            recv_sem=tok_recv.at[k, h],
            device_id={"tp": z + by},
            device_id_type=MESH,
        )

    def send_own(h):
        @pl.when(z + 1 < ntp)
        def _():
            tok_copy(z, h, 1, tok_right, True).start()

        @pl.when(z > 0)
        def _():
            tok_copy(z, h, -1, tok_left, True).start()

    def take(d, h):
        @pl.when(z - d >= 0)
        def _():
            tok_copy(z - d, h, 1, tok_right, False).wait_recv()

            @pl.when(z + 1 < ntp)
            def _():
                tok_copy(z - d, h, 1, tok_right, False).start()

        @pl.when(z + d < ntp)
        def _():
            tok_copy(z + d, h, -1, tok_left, False).wait_recv()

            @pl.when(z > 0)
            def _():
                tok_copy(z + d, h, -1, tok_left, False).start()

    tn = min(512, width)
    blocks = width // tn

    def multiply(k, i, first):
        if i == 0:
            w_copy(k).wait()
        part_k = pl.ds(pl.multiple_of(k * depth, depth), depth)
        at = pl.ds(i * tn, tn)
        got = jnp.dot(tok_all[k], w_ref[part_k, at], preferred_element_type=f32)
        acc[:, at] = got if first else acc[:, at] + got

    def multiply_pair(d, i):
        @pl.when(z - d >= 0)
        def _():
            multiply(z - d, i, False)

        @pl.when(z + d < ntp)
        def _():
            multiply(z + d, i, False)

    halo = pltpu.make_async_remote_copy(
        src_ref=halo_out,
        dst_ref=halo_in,
        send_sem=halo_sem.at[0],
        recv_sem=halo_sem.at[1],
        device_id={"seq": q + 1},
        device_id_type=MESH,
    )

    def rs_copy(p, d):
        to = lax.rem(z + d, ntp)
        return pltpu.make_async_remote_copy(
            src_ref=ps.at[p, to],
            dst_ref=rs.at[p, d - 1],
            send_sem=rs_send.at[p, d - 1],
            recv_sem=rs_recv.at[p, d - 1],
            device_id={"tp": to},
            device_id_type=MESH,
        )

    def ag_copy(p, d):
        to = lax.rem(z + d, ntp)
        return pltpu.make_async_remote_copy(
            src_ref=ag.at[p, z],
            dst_ref=ag.at[p, z],
            send_sem=ag_send.at[p, d - 1],
            recv_sem=ag_recv.at[p, d - 1],
            device_id={"tp": to},
            device_id_type=MESH,
        )

    def project(p):
        r0 = phase_rows[p]

        @pl.loop(0, tiles)
        def _(j):
            at = tile_at(j)
            pre = cb_ref[:, at] + cw_ref[0:1, at] * pad[pl.ds(r0 + 9 - taps, half), at]
            for k in range(1, taps):
                pre = pre + cw_ref[k : k + 1, at] * pad[pl.ds(r0 + 9 - taps + k, half), at]
            u_ref[pl.ds(r0, half), at] = (pre * sigmoid(pre)).astype(bf16)

        sums = lax.dot_general(
            u_ref[pl.ds(r0, half), :],
            proj_ref[...],
            (((1,), (1,)), ((), ())),
            preferred_element_type=f32,
        )
        for k in range(ntp):
            mine = sums[k * per : (k + 1) * per]
            part[p, k, :, :cols] = mine
            ps[p, k, :, :cols] = mine.astype(ps.dtype)
        for d in range(1, ntp):
            rs_copy(p, d).start()

    def reduce(p):
        red = part[p, z]
        for d in range(1, ntp):
            rs_copy(p, d).wait_recv()
            red = red + rs[p, d - 1].astype(f32)
        ag[p, z] = red.astype(ag.dtype)
        for d in range(1, ntp):
            ag_copy(p, d).start()

    two = 2 * n_state

    def prepare(p):
        r0 = phase_rows[p]
        mine = pl.ds(r0, half)
        for d in range(1, ntp):
            ag_copy(p, d).wait_recv()
        for k in range(ntp):
            tot[pl.ds(r0 + k * per, per), :] = ag[p, k].astype(f32)
        dt_low = tot[mine, :rank].astype(bf16)

        @pl.loop(0, width // tn)
        def _(s):
            at = pl.ds(pl.multiple_of(s * tn, tn), tn)
            v = jnp.dot(dt_low, dtw_ref[:, at], preferred_element_type=f32) + dtb_ref[:, at]
            e = jnp.exp(-jnp.abs(v))
            e = jnp.where(e < 1e-3, e - (0.5 * e) * e, jnp.log(1.0 + e))
            v = jnp.maximum(v, 0.0) + e
            flow = v * u_ref[mine, at].astype(f32)
            for i in range(tn // LANES):
                cut = slice(i * LANES, (i + 1) * LANES)
                to = pl.ds(r0 * stride + s * (tn // LANES) + i, half, stride=stride)
                dt3[to, :] = v[:, cut]
                du3[to, :] = flow[:, cut]

        for n in range(two):
            bs[pl.ds(n * rows + r0, half), :] = jnp.broadcast_to(
                tot[mine, rank + n : rank + n + 1], (half, LANES)
            )

    def rates(g):
        return [
            r3[pl.ds(pl.multiple_of(n * stride + g * 8, 8), 8), :] for n in range(n_state)
        ]

    def splat(t, n):
        return bs[pl.ds(n * rows + t, 8, stride=0), :]

    def st_copy(g, d):
        return pltpu.make_async_remote_copy(
            src_ref=sx.at[g],
            dst_ref=sr.at[g, d - 1],
            send_sem=st_send.at[g, d - 1],
            recv_sem=st_recv.at[g, d - 1],
            device_id={"seq": q + d},
            device_id_type=MESH,
        )

    def first_pass(p, g):
        rate = rates(g)
        r0 = phase_rows[p]

        def step(t, carry):
            states, total = carry
            at = pl.ds(pl.multiple_of(t * stride + g * 8, 8), 8)
            dt, du = dt3[at, :], du3[at, :]
            states = [
                jnp.exp2(dt * rate[n]) * states[n] + du * splat(t, n) for n in range(n_state)
            ]
            return states, total + dt

        zero = jnp.zeros((8, LANES), f32)
        states, total = lax.fori_loop(
            r0, r0 + half, step, ([zero] * n_state, zero), unroll=16
        )
        if p == 0:
            for n in range(n_state):
                later[g, pl.ds(n * 8, 8), :] = states[n]
            later[g, pl.ds(n_state * 8, 8), :] = total
            return
        more = later[g, pl.ds(n_state * 8, 8), :]
        states = [
            jnp.exp2(more * rate[n]) * states[n] + later[g, pl.ds(n * 8, 8), :]
            for n in range(n_state)
        ]
        total = total + more
        high = total.astype(bf16).astype(f32)
        items = states + [high, total - high]
        for n in range(0, len(items), 2):
            sx[g, pl.ds(n * 8, 16), :] = jnp.concatenate(items[n : n + 2], axis=0).astype(bf16)
        for d in range(1, ns):

            @pl.when(q + d < ns)
            def _():
                st_copy(g, d).start()

    def second_pass(g):
        rate = rates(g)
        zero = jnp.zeros((8, LANES), f32)
        for n in range(n_state):
            entry[pl.ds(n * 8, 8), :] = zero
        for d in range(ns - 1, 0, -1):

            @pl.when(q - d >= 0)
            def _():
                st_copy(g, d).wait_recv()
                sums = sr[g, d - 1, pl.ds(n_state * 8, 16), :].astype(f32)
                sums = sums[:8] + sums[8:]
                for n in range(0, n_state, 2):
                    ends = sr[g, d - 1, pl.ds(n * 8, 16), :].astype(f32)
                    for i in range(2):
                        at = pl.ds((n + i) * 8, 8)
                        entry[at, :] = (
                            jnp.exp2(sums * rate[n + i]) * entry[at, :] + ends[i * 8 : i * 8 + 8]
                        )

        def step(t, states):
            at = pl.ds(pl.multiple_of(t * stride + g * 8, 8), 8)
            dt, du = dt3[at, :], du3[at, :]
            states = [
                jnp.exp2(dt * rate[n]) * states[n] + du * splat(t, n) for n in range(n_state)
            ]
            terms = [splat(t, n_state + n) * states[n] for n in range(n_state)]
            while len(terms) > 1:
                terms = [a + b for a, b in zip(terms[::2], terms[1::2])]
            y3[at, :] = terms[0]
            return states

        lax.fori_loop(0, rows, step, [entry[pl.ds(n * 8, 8), :] for n in range(n_state)], unroll=16)

        @pl.loop(g * 8, jnp.minimum(g * 8 + 8, tiles))
        def _(j):
            at = tile_at(j)
            y = y3[pl.ds(j, rows, stride=stride), :] + skip_ref[:, at] * u_ref[:, at].astype(f32)
            out_ref[:, at] = (y * sigmoid(4.0 * (y - thr_ref[:, at]))).astype(bf16)

    for h in range(PIECES):
        send_own(h)
    in_copy(8).wait()
    in_copy(5).wait()
    for j in range(tiles):
        at = slice(j * LANES, (j + 1) * LANES)
        r3[pl.ds(j, n_state, stride=stride), :] = -LOG2E * jnp.exp(alog_ref[:, at])
    part[:, :, :, cols:] = jnp.zeros(part.shape[:3] + (part.shape[3] - cols,), f32)
    ps[:, :, :, cols:] = jnp.zeros(ps.shape[:3] + (ps.shape[3] - cols,), ps.dtype)
    for h in range(PIECES):
        if ntp > 1:
            take(1, h)
        for i in range(h, blocks, PIECES):
            multiply(z, i, True)

    @pl.loop(2, ntp)
    def _(d):
        for h in range(PIECES):
            take(d, h)
            for i in range(h, blocks, PIECES):
                multiply_pair(d - 1, i)

    if ntp > 1:
        for i in range(blocks):
            multiply_pair(ntp - 1, i)
    halo_out[...] = acc[rows - 16 :, :].astype(bf16)

    @pl.when(q + 1 < ns)
    def _():
        halo.start()

    pad[pl.ds(8, rows), :] = acc[...].astype(bf16).astype(f32)
    for i in (0, 1, 2):
        in_copy(i).wait()
    project(0)

    @pl.when(q > 0)
    def _():
        halo.wait_recv()
        pad[pl.ds(0, 8), :] = halo_in[...].astype(f32)[8:]

    @pl.when(q == 0)
    def _():
        pad[pl.ds(0, 8), :] = jnp.zeros((8, width), f32)

    project(1)
    reduce(0)
    reduce(1)

    in_copy(3).wait()
    in_copy(4).wait()
    prepare(0)

    @pl.loop(0, groups)
    def _(g):
        first_pass(0, g)

    prepare(1)

    @pl.loop(0, groups)
    def _(g):
        first_pass(1, g)

    in_copy(6).wait()
    in_copy(7).wait()

    @pl.loop(0, groups)
    def _(g):
        second_pass(g)


    for k in range(ntp):
        for h in range(PIECES):

            @pl.when((z + 1 < ntp) & (k <= z))
            def _():
                tok_copy(k, h, 1, tok_right, False).wait_send()

            @pl.when((z > 0) & (k >= z))
            def _():
                tok_copy(k, h, -1, tok_left, False).wait_send()

    @pl.when(q + 1 < ns)
    def _():
        halo.wait_send()

    for p in range(2):
        for d in range(1, ntp):
            rs_copy(p, d).wait_send()
            ag_copy(p, d).wait_send()
    for g in range(groups):
        for d in range(1, ns):

            @pl.when(q + d < ns)
            def _():
                st_copy(g, d).wait_send()


def per_device(
    ns,
    ntp,
    tokens,
    in_weight,
    conv_weight,
    conv_bias,
    proj_weight,
    dt_weight,
    dt_bias,
    a_log,
    skip_gain,
    threshold,
):
    rows, depth = tokens.shape
    width = in_weight.shape[1]
    n_state = a_log.shape[0]
    stride = -(-width // (8 * LANES)) * 8
    groups = stride // 8
    padded = -(-proj_weight.shape[1] // LANES) * LANES
    per = rows // 2 // ntp
    f32, bf16 = jnp.float32, jnp.bfloat16
    sent = bf16 if per % 16 == 0 else f32
    dma = pltpu.SemaphoreType.DMA
    vmem = pl.BlockSpec(memory_space=pltpu.VMEM)
    return pl.pallas_call(
        functools.partial(kernel, ns, ntp),
        out_shape=jax.ShapeDtypeStruct((rows, width), bf16),
        in_specs=[pl.BlockSpec(memory_space=pl.ANY)] * 10,
        out_specs=vmem,
        scratch_shapes=[
            pltpu.VMEM(in_weight.shape, bf16),
            pltpu.VMEM(conv_weight.shape, f32),
            pltpu.VMEM((1, width), f32),
            pltpu.VMEM(proj_weight.shape[::-1], bf16),
            pltpu.VMEM(dt_weight.shape, bf16),
            pltpu.VMEM((1, width), f32),
            pltpu.VMEM(a_log.shape, f32),
            pltpu.VMEM((1, width), f32),
            pltpu.VMEM((1, width), f32),
            pltpu.VMEM((ntp, rows, depth), bf16),
            pltpu.VMEM((rows, width), f32),
            pltpu.VMEM((rows + 8, width), f32),
            pltpu.VMEM((16, width), bf16),
            pltpu.VMEM((16, width), bf16),
            pltpu.VMEM((rows, width), bf16),
            pltpu.VMEM((2, ntp, per, padded), f32),
            pltpu.VMEM((2, ntp, per, padded), sent),
            pltpu.VMEM((2, ntp - 1, per, padded), sent),
            pltpu.VMEM((2, ntp, per, padded), sent),
            pltpu.VMEM((rows, padded), f32),
            pltpu.VMEM((rows * 2 * n_state + 8, LANES), f32),
            pltpu.VMEM((rows * stride, LANES), f32),
            pltpu.VMEM((rows * stride, LANES), f32),
            pltpu.VMEM((rows * stride, LANES), f32),
            pltpu.VMEM((n_state * stride, LANES), f32),
            pltpu.VMEM((groups, n_state * 8 + 8, LANES), f32),
            pltpu.VMEM((groups, n_state * 8 + 16, LANES), bf16),
            pltpu.VMEM((groups, ns - 1, n_state * 8 + 16, LANES), bf16),
            pltpu.VMEM((n_state * 8, LANES), f32),
            dma((ntp,)),
            dma((9,)),
            dma((ntp, PIECES)),
            dma((ntp, PIECES)),
            dma((ntp, PIECES)),
            dma((2,)),
            dma((2, ntp - 1)),
            dma((2, ntp - 1)),
            dma((2, ntp - 1)),
            dma((2, ntp - 1)),
            dma((groups, ns - 1)),
            dma((groups, ns - 1)),
        ],
        compiler_params=pltpu.CompilerParams(
            collective_id=0, has_side_effects=True, vmem_limit_bytes=63 * 1024 * 1024
        ),
    )(
        tokens,
        in_weight,
        conv_weight,
        conv_bias.reshape(1, -1),
        proj_weight.T,
        dt_weight,
        dt_bias.reshape(1, -1),
        a_log,
        skip_gain.reshape(1, -1),
        threshold.reshape(1, -1),
    )


def solution(mesh):
    return jax.shard_map(
        functools.partial(per_device, mesh.shape["seq"], mesh.shape["tp"]),
        mesh=mesh,
        in_specs=(
            P("seq", "tp"),
            P(None, "tp"),
            P(None, "tp"),
            P("tp"),
            P("tp", None),
            P(None, "tp"),
            P("tp"),
            P(None, "tp"),
            P("tp"),
            P("tp"),
        ),
        out_specs=P("seq", "tp"),
        check_vma=False,
    )
```

```python
import functools

import jax
import jax.numpy as jnp
from jax import lax
from jax.experimental import pallas as pl
from jax.experimental.pallas import tpu as pltpu
from jax.sharding import PartitionSpec as P

MESH = pl.DeviceIdType.MESH
LOG2E = 1.4426950408889634
LANES = 128


def kernel(
    ns,
    ntp,
    tok_hbm,
    w_hbm,
    cw_hbm,
    cb_hbm,
    proj_hbm,
    dtw_hbm,
    dtb_hbm,
    alog_hbm,
    skip_hbm,
    thr_hbm,
    out_ref,
    w_ref,
    cw_ref,
    cb_ref,
    proj_ref,
    dtw_ref,
    dtb_ref,
    alog_ref,
    skip_ref,
    thr_ref,
    tok_all,
    acc,
    pad,
    halo_out,
    halo_in,
    u_ref,
    part,
    ps,
    rs,
    ag,
    tot,
    bs,
    dt3,
    du3,
    y3,
    r3,
    later,
    sx,
    sr,
    entry,
    w_sem,
    in_sem,
    tok_recv,
    tok_right,
    tok_left,
    halo_sem,
    rs_send,
    rs_recv,
    ag_send,
    ag_recv,
    st_send,
    st_recv,
):
    q = lax.axis_index("seq")
    z = lax.axis_index("tp")
    rows, depth = tok_hbm.shape
    width = w_ref.shape[1]
    taps = cw_ref.shape[0]
    rank = dtw_ref.shape[0]
    n_state = alog_ref.shape[0]
    cols = proj_ref.shape[0]
    tiles = width // LANES
    stride = r3.shape[0] // n_state
    groups = stride // 8
    per = ag.shape[2]
    f32, bf16 = jnp.float32, jnp.bfloat16
    half = rows // 2
    pieces, piece = tok_all.shape[1], tok_all.shape[3]
    phase_rows = (half, 0)

    small = [
        (cw_hbm, cw_ref),
        (cb_hbm, cb_ref),
        (proj_hbm, proj_ref),
        (dtw_hbm, dtw_ref),
        (dtb_hbm, dtb_ref),
        (alog_hbm, alog_ref),
        (skip_hbm, skip_ref),
        (thr_hbm, thr_ref),
    ]
    for h in range(tok_all.shape[1]):
        part_h = pl.ds(h * tok_all.shape[3], tok_all.shape[3])
        small.append((tok_hbm.at[:, part_h], tok_all.at[z, h]))

    def tile_at(j):
        return pl.ds(pl.multiple_of(j * LANES, LANES), LANES)

    def sigmoid(v):
        return 0.5 + 0.5 * jnp.tanh(0.5 * v)

    def in_copy(i):
        return pltpu.make_async_copy(small[i][0], small[i][1], in_sem.at[i])

    def w_copy(k):
        part_k = pl.ds(pl.multiple_of(k * depth, depth), depth)
        return pltpu.make_async_copy(w_hbm.at[part_k], w_ref.at[part_k], w_sem.at[k])

    for h in range(pieces):
        in_copy(8 + h).start()
    w_copy(z).start()

    barrier = pltpu.get_barrier_semaphore()
    for d in range(1, ntp):
        pl.semaphore_signal(
            barrier, inc=1, device_id={"tp": lax.rem(z + d, ntp)}, device_id_type=MESH
        )
    for d in range(1, ns):
        pl.semaphore_signal(
            barrier, inc=1, device_id={"seq": lax.rem(q + d, ns)}, device_id_type=MESH
        )
    for i in (5, 0, 1, 2, 3, 4, 6, 7):
        in_copy(i).start()
    for i in range(1, ntp):
        w_copy(lax.rem(z + i, ntp)).start()
    pl.semaphore_wait(barrier, ns + ntp - 2)

    def tok_copy(k, h, by, sems, own):
        at = pl.ds(h * piece, piece)
        return pltpu.make_async_remote_copy(
            src_ref=tok_hbm.at[:, at] if own else tok_all.at[k, h],
            dst_ref=tok_all.at[k, h],
            send_sem=sems.at[k, h],
            recv_sem=tok_recv.at[k, h],
            device_id={"tp": z + by},
            device_id_type=MESH,
        )

    def send_own(h):
        @pl.when(z + 1 < ntp)
        def _():
            tok_copy(z, h, 1, tok_right, True).start()

        @pl.when(z > 0)
        def _():
            tok_copy(z, h, -1, tok_left, True).start()

    def take(d, h):
        @pl.when(z - d >= 0)
        def _():
            tok_copy(z - d, h, 1, tok_right, False).wait_recv()

            @pl.when(z + 1 < ntp)
            def _():
                tok_copy(z - d, h, 1, tok_right, False).start()

        @pl.when(z + d < ntp)
        def _():
            tok_copy(z + d, h, -1, tok_left, False).wait_recv()

            @pl.when(z > 0)
            def _():
                tok_copy(z + d, h, -1, tok_left, False).start()

    tn = min(512, width)
    blocks = width // tn

    def multiply(k, h, first):
        if h == 0:
            w_copy(k).wait()
        part_k = pl.ds(pl.multiple_of(k * depth + h * piece, piece), piece)
        for i in range(blocks):
            at = pl.ds(i * tn, tn)
            got = jnp.dot(tok_all[k, h], w_ref[part_k, at], preferred_element_type=f32)
            acc[:, at] = got if first else acc[:, at] + got

    def multiply_pair(d, h):
        @pl.when(z - d >= 0)
        def _():
            multiply(z - d, h, False)

        @pl.when(z + d < ntp)
        def _():
            multiply(z + d, h, False)

    halo = pltpu.make_async_remote_copy(
        src_ref=halo_out,
        dst_ref=halo_in,
        send_sem=halo_sem.at[0],
        recv_sem=halo_sem.at[1],
        device_id={"seq": q + 1},
        device_id_type=MESH,
    )

    def rs_copy(p, d):
        to = lax.rem(z + d, ntp)
        return pltpu.make_async_remote_copy(
            src_ref=ps.at[p, to],
            dst_ref=rs.at[p, d - 1],
            send_sem=rs_send.at[p, d - 1],
            recv_sem=rs_recv.at[p, d - 1],
            device_id={"tp": to},
            device_id_type=MESH,
        )

    def ag_copy(p, d):
        to = lax.rem(z + d, ntp)
        return pltpu.make_async_remote_copy(
            src_ref=ag.at[p, z],
            dst_ref=ag.at[p, z],
            send_sem=ag_send.at[p, d - 1],
            recv_sem=ag_recv.at[p, d - 1],
            device_id={"tp": to},
            device_id_type=MESH,
        )

    def project(p):
        r0 = phase_rows[p]

        @pl.loop(0, tiles)
        def _(j):
            at = tile_at(j)
            pre = cb_ref[:, at] + cw_ref[0:1, at] * pad[pl.ds(r0 + 9 - taps, half), at]
            for k in range(1, taps):
                pre = pre + cw_ref[k : k + 1, at] * pad[pl.ds(r0 + 9 - taps + k, half), at]
            u_ref[pl.ds(r0, half), at] = (pre * sigmoid(pre)).astype(bf16)

        sums = lax.dot_general(
            u_ref[pl.ds(r0, half), :],
            proj_ref[...],
            (((1,), (1,)), ((), ())),
            preferred_element_type=f32,
        )
        for k in range(ntp):
            mine = sums[k * per : (k + 1) * per]
            part[p, k, :, :cols] = mine
            ps[p, k, :, :cols] = mine.astype(ps.dtype)
        for d in range(1, ntp):
            rs_copy(p, d).start()

    def reduce(p):
        red = part[p, z]
        for d in range(1, ntp):
            rs_copy(p, d).wait_recv()
            red = red + rs[p, d - 1].astype(f32)
        ag[p, z] = red.astype(ag.dtype)
        for d in range(1, ntp):
            ag_copy(p, d).start()

    two = 2 * n_state

    def prepare(p):
        r0 = phase_rows[p]
        mine = pl.ds(r0, half)
        for d in range(1, ntp):
            ag_copy(p, d).wait_recv()
        for k in range(ntp):
            tot[pl.ds(r0 + k * per, per), :] = ag[p, k].astype(f32)
        dt_low = tot[mine, :rank].astype(bf16)

        @pl.loop(0, width // tn)
        def _(s):
            at = pl.ds(pl.multiple_of(s * tn, tn), tn)
            v = jnp.dot(dt_low, dtw_ref[:, at], preferred_element_type=f32) + dtb_ref[:, at]
            e = jnp.exp(-jnp.abs(v))
            e = jnp.where(e < 1e-3, e - (0.5 * e) * e, jnp.log(1.0 + e))
            v = jnp.maximum(v, 0.0) + e
            flow = v * u_ref[mine, at].astype(f32)
            for i in range(tn // LANES):
                cut = slice(i * LANES, (i + 1) * LANES)
                to = pl.ds(r0 * stride + s * (tn // LANES) + i, half, stride=stride)
                dt3[to, :] = v[:, cut]
                du3[to, :] = flow[:, cut]

        for n in range(two):
            bs[pl.ds(n * rows + r0, half), :] = jnp.broadcast_to(
                tot[mine, rank + n : rank + n + 1], (half, LANES)
            )

    def rates(g):
        return [
            r3[pl.ds(pl.multiple_of(n * stride + g * 8, 8), 8), :] for n in range(n_state)
        ]

    def splat(t, n):
        return bs[pl.ds(n * rows + t, 8, stride=0), :]

    def st_copy(g, d):
        return pltpu.make_async_remote_copy(
            src_ref=sx.at[g],
            dst_ref=sr.at[g, d - 1],
            send_sem=st_send.at[g, d - 1],
            recv_sem=st_recv.at[g, d - 1],
            device_id={"seq": q + d},
            device_id_type=MESH,
        )

    def first_pass(p, g):
        rate = rates(g)
        r0 = phase_rows[p]

        def step(t, carry):
            states, total = carry
            at = pl.ds(pl.multiple_of(t * stride + g * 8, 8), 8)
            dt, du = dt3[at, :], du3[at, :]
            states = [
                jnp.exp2(dt * rate[n]) * states[n] + du * splat(t, n) for n in range(n_state)
            ]
            return states, total + dt

        zero = jnp.zeros((8, LANES), f32)
        states, total = lax.fori_loop(
            r0, r0 + half, step, ([zero] * n_state, zero), unroll=16
        )
        if p == 0:
            for n in range(n_state):
                later[g, pl.ds(n * 8, 8), :] = states[n]
            later[g, pl.ds(n_state * 8, 8), :] = total
            return
        more = later[g, pl.ds(n_state * 8, 8), :]
        states = [
            jnp.exp2(more * rate[n]) * states[n] + later[g, pl.ds(n * 8, 8), :]
            for n in range(n_state)
        ]
        total = total + more
        high = total.astype(bf16).astype(f32)
        items = states + [high, total - high]
        for n in range(0, len(items), 2):
            sx[g, pl.ds(n * 8, 16), :] = jnp.concatenate(items[n : n + 2], axis=0).astype(bf16)
        for d in range(1, ns):

            @pl.when(q + d < ns)
            def _():
                st_copy(g, d).start()

    def second_pass(g):
        rate = rates(g)
        zero = jnp.zeros((8, LANES), f32)
        for n in range(n_state):
            entry[pl.ds(n * 8, 8), :] = zero
        for d in range(ns - 1, 0, -1):

            @pl.when(q - d >= 0)
            def _():
                st_copy(g, d).wait_recv()
                sums = sr[g, d - 1, pl.ds(n_state * 8, 16), :].astype(f32)
                sums = sums[:8] + sums[8:]
                for n in range(0, n_state, 2):
                    ends = sr[g, d - 1, pl.ds(n * 8, 16), :].astype(f32)
                    for i in range(2):
                        at = pl.ds((n + i) * 8, 8)
                        entry[at, :] = (
                            jnp.exp2(sums * rate[n + i]) * entry[at, :] + ends[i * 8 : i * 8 + 8]
                        )

        def step(t, states):
            at = pl.ds(pl.multiple_of(t * stride + g * 8, 8), 8)
            dt, du = dt3[at, :], du3[at, :]
            states = [
                jnp.exp2(dt * rate[n]) * states[n] + du * splat(t, n) for n in range(n_state)
            ]
            terms = [splat(t, n_state + n) * states[n] for n in range(n_state)]
            while len(terms) > 1:
                terms = [a + b for a, b in zip(terms[::2], terms[1::2])]
            y3[at, :] = terms[0]
            return states

        lax.fori_loop(0, rows, step, [entry[pl.ds(n * 8, 8), :] for n in range(n_state)], unroll=16)

        @pl.loop(g * 8, jnp.minimum(g * 8 + 8, tiles))
        def _(j):
            at = tile_at(j)
            y = y3[pl.ds(j, rows, stride=stride), :] + skip_ref[:, at] * u_ref[:, at].astype(f32)
            out_ref[:, at] = (y * sigmoid(4.0 * (y - thr_ref[:, at]))).astype(bf16)

    for h in range(pieces):
        send_own(h)
    in_copy(5).wait()
    for j in range(tiles):
        at = slice(j * LANES, (j + 1) * LANES)
        r3[pl.ds(j, n_state, stride=stride), :] = -LOG2E * jnp.exp(alog_ref[:, at])
    part[:, :, :, cols:] = jnp.zeros(part.shape[:3] + (part.shape[3] - cols,), f32)
    ps[:, :, :, cols:] = jnp.zeros(ps.shape[:3] + (ps.shape[3] - cols,), ps.dtype)
    for h in range(pieces):
        in_copy(8 + h).wait()
        multiply(z, h, h == 0)
        if ntp > 2:
            take(1, h)

    @pl.loop(2, ntp - 1)
    def _(d):
        for h in range(pieces):
            multiply_pair(d - 1, h)
            take(d, h)

    for h in range(pieces):
        if ntp > 2:
            multiply_pair(ntp - 2, h)
    for h in range(pieces):
        if ntp > 1:
            take(ntp - 1, h)
            multiply_pair(ntp - 1, h)
    halo_out[...] = acc[rows - 16 :, :].astype(bf16)

    @pl.when(q + 1 < ns)
    def _():
        halo.start()

    pad[pl.ds(8, rows), :] = acc[...].astype(bf16).astype(f32)
    for i in (0, 1, 2):
        in_copy(i).wait()
    project(0)

    @pl.when(q > 0)
    def _():
        halo.wait_recv()
        pad[pl.ds(0, 8), :] = halo_in[...].astype(f32)[8:]

    @pl.when(q == 0)
    def _():
        pad[pl.ds(0, 8), :] = jnp.zeros((8, width), f32)

    project(1)
    reduce(0)
    reduce(1)

    in_copy(3).wait()
    in_copy(4).wait()
    prepare(0)

    @pl.loop(0, groups)
    def _(g):
        first_pass(0, g)

    prepare(1)

    @pl.loop(0, groups)
    def _(g):
        first_pass(1, g)

    in_copy(6).wait()
    in_copy(7).wait()

    @pl.loop(0, groups)
    def _(g):
        second_pass(g)


    for k in range(ntp):
        for h in range(pieces):

            @pl.when((z + 1 < ntp) & (k <= z))
            def _():
                tok_copy(k, h, 1, tok_right, False).wait_send()

            @pl.when((z > 0) & (k >= z))
            def _():
                tok_copy(k, h, -1, tok_left, False).wait_send()

    @pl.when(q + 1 < ns)
    def _():
        halo.wait_send()

    for p in range(2):
        for d in range(1, ntp):
            rs_copy(p, d).wait_send()
            ag_copy(p, d).wait_send()
    for g in range(groups):
        for d in range(1, ns):

            @pl.when(q + d < ns)
            def _():
                st_copy(g, d).wait_send()


def per_device(
    ns,
    ntp,
    tokens,
    in_weight,
    conv_weight,
    conv_bias,
    proj_weight,
    dt_weight,
    dt_bias,
    a_log,
    skip_gain,
    threshold,
):
    rows, depth = tokens.shape
    width = in_weight.shape[1]
    n_state = a_log.shape[0]
    stride = -(-width // (8 * LANES)) * 8
    groups = stride // 8
    padded = -(-proj_weight.shape[1] // LANES) * LANES
    per = rows // 2 // ntp
    pieces = max(1, depth // 256)
    f32, bf16 = jnp.float32, jnp.bfloat16
    sent = bf16 if per % 16 == 0 else f32
    dma = pltpu.SemaphoreType.DMA
    vmem = pl.BlockSpec(memory_space=pltpu.VMEM)
    return pl.pallas_call(
        functools.partial(kernel, ns, ntp),
        out_shape=jax.ShapeDtypeStruct((rows, width), bf16),
        in_specs=[pl.BlockSpec(memory_space=pl.ANY)] * 10,
        out_specs=vmem,
        scratch_shapes=[
            pltpu.VMEM(in_weight.shape, bf16),
            pltpu.VMEM(conv_weight.shape, f32),
            pltpu.VMEM((1, width), f32),
            pltpu.VMEM(proj_weight.shape[::-1], bf16),
            pltpu.VMEM(dt_weight.shape, bf16),
            pltpu.VMEM((1, width), f32),
            pltpu.VMEM(a_log.shape, f32),
            pltpu.VMEM((1, width), f32),
            pltpu.VMEM((1, width), f32),
            pltpu.VMEM((ntp, pieces, rows, depth // pieces), bf16),
            pltpu.VMEM((rows, width), f32),
            pltpu.VMEM((rows + 8, width), f32),
            pltpu.VMEM((16, width), bf16),
            pltpu.VMEM((16, width), bf16),
            pltpu.VMEM((rows, width), bf16),
            pltpu.VMEM((2, ntp, per, padded), f32),
            pltpu.VMEM((2, ntp, per, padded), sent),
            pltpu.VMEM((2, ntp - 1, per, padded), sent),
            pltpu.VMEM((2, ntp, per, padded), sent),
            pltpu.VMEM((rows, padded), f32),
            pltpu.VMEM((rows * 2 * n_state + 8, LANES), f32),
            pltpu.VMEM((rows * stride, LANES), f32),
            pltpu.VMEM((rows * stride, LANES), f32),
            pltpu.VMEM((rows * stride, LANES), f32),
            pltpu.VMEM((n_state * stride, LANES), f32),
            pltpu.VMEM((groups, n_state * 8 + 8, LANES), f32),
            pltpu.VMEM((groups, n_state * 8 + 16, LANES), bf16),
            pltpu.VMEM((groups, ns - 1, n_state * 8 + 16, LANES), bf16),
            pltpu.VMEM((n_state * 8, LANES), f32),
            dma((ntp,)),
            dma((8 + pieces,)),
            dma((ntp, pieces)),
            dma((ntp, pieces)),
            dma((ntp, pieces)),
            dma((2,)),
            dma((2, ntp - 1)),
            dma((2, ntp - 1)),
            dma((2, ntp - 1)),
            dma((2, ntp - 1)),
            dma((groups, ns - 1)),
            dma((groups, ns - 1)),
        ],
        compiler_params=pltpu.CompilerParams(
            collective_id=0, has_side_effects=True, vmem_limit_bytes=63 * 1024 * 1024
        ),
    )(
        tokens,
        in_weight,
        conv_weight,
        conv_bias.reshape(1, -1),
        proj_weight.T,
        dt_weight,
        dt_bias.reshape(1, -1),
        a_log,
        skip_gain.reshape(1, -1),
        threshold.reshape(1, -1),
    )


def solution(mesh):
    return jax.shard_map(
        functools.partial(per_device, mesh.shape["seq"], mesh.shape["tp"]),
        mesh=mesh,
        in_specs=(
            P("seq", "tp"),
            P(None, "tp"),
            P(None, "tp"),
            P("tp"),
            P("tp", None),
            P(None, "tp"),
            P("tp"),
            P(None, "tp"),
            P("tp"),
            P("tp"),
        ),
        out_specs=P("seq", "tp"),
        check_vma=False,
    )
```
